32 devices in a mesh: row: 8 (over y, x, core), col: 4 (over z).
Axes of the slice: x: 2, y: 2, z: 4, core: 2. Of those that a mesh axis runs over, the one named last changes fastest.
Arguments:
- inputs: bfloat16 [768, 12288], P('row', 'col'), may hold values from -6 to 6
- first_values: bfloat16 [96, 96, 128, 128], P('col', 'row'), may hold values from -0.109375 to 0.109375
- first_blocks: int32 [96, 96], P('col', 'row'), may hold values from 0 to 383, as said below
- second_values: bfloat16 [384, 24, 128, 128], P('row', 'col'), may hold values from -0.0546875 to 0.0546875
- second_blocks: int32 [384, 24], P('row', 'col'), may hold values from 0 to 95, as said below
- cotangent: bfloat16 [768, 12288], P('row', 'col'), may hold values from -6 to 6
Outputs:
- outputs: bfloat16 [768, 12288], P('row', 'col')
- input_grad: bfloat16 [768, 12288], P('row', 'col')
- first_grad: bfloat16 [96, 96, 128, 128], P('col', 'row')
- second_grad: bfloat16 [384, 24, 128, 128], P('row', 'col')
The draws below stay inside these ranges and needn't reach their ends.
Inputs may be any that keep to these rules, and one draw needn't show every extreme that they name: `first_blocks`: in block row i, slots g * 12 to (g + 1) * 12 - 1 name 12 different column blocks in increasing order, all within 4 * g * 12 to 4 * (g + 1) * 12 - 1. `second_blocks`: in block row j, slots g * 6 to (g + 1) * 6 - 1 name 6 different column blocks in increasing order, all within 4 * g * 6 to 4 * (g + 1) * 6 - 1.
All inputs are finite; a program needn't handle non-finite values.
Results may differ from the reference program's by a relative error of at most 0.0049.
Values may be sent and summed in bfloat16 or wider, within the bound.
No kernel may reach another device: no remote copies, remote signals or barrier semaphores. Data moves between devices by JAX's collectives and lax.ppermute only.
A program may use at most 256 MiB of HBM per device.

```python
import jax
import jax.numpy as jnp
from jax import lax

D = 12288
F = 49152
BLK = 128
TOKENS = 768
S1 = 12
S2 = 6
N_ROW = 8
N_COL = 4


def pick_blocks(key, block_rows, groups, chosen):
    group_span = 4 * chosen
    key_list = jax.random.split(key, block_rows * groups)

    def one_list(single):
        return jnp.sort(jax.random.permutation(single, group_span)[:chosen])
    chosen_lists = jax.vmap(one_list)(key_list).reshape(block_rows, groups, chosen)
    offsets = (jnp.arange(groups, dtype=jnp.int32) * group_span)[None, :, None]
    return (chosen_lists.astype(jnp.int32) + offsets).reshape(block_rows, groups * chosen).astype(jnp.int32)


def draw_first_blocks(key, part):
    key = jax.random.fold_in(key, 11)
    return pick_blocks(key, D // BLK, F // BLK // (4 * S1), S1)


def draw_second_blocks(key, part):
    key = jax.random.fold_in(key, 23)
    return pick_blocks(key, F // BLK, D // BLK // (4 * S2), S2)


def level_of(own_key, shape, cuts, smallest, top_value):
    factor_of = 1.0
    for dim, shards_of in cuts:
        heights = jax.random.uniform(jax.random.fold_in(jax.random.fold_in(own_key, 6), dim), (shards_of,), jnp.float32, smallest / len(cuts), top_value / len(cuts))
        factor_of = factor_of * jnp.repeat(jnp.exp(heights), shape[dim] // shards_of).reshape((-1,) + (1,) * (len(shape) - 1 - dim))
    return factor_of


def bell_draw(key, dims, scale, reach, shards=(), kind=jnp.bfloat16):
    entries = jax.random.normal(key, dims, jnp.float32) * scale
    if len(shards) > 0:
        entries = level_of(key, dims, shards, -0.22, 0.18) * entries
    return jnp.clip(entries, min=-reach, max=reach).astype(kind)


def setup_inputs(seed: int = 0) -> dict:
    splits = jax.random.split(jax.random.key(seed), 7)
    return {
        "inputs": bell_draw(splits[0], (TOKENS, D), 1.0, 6.0, ((0, 8), (1, 4))),
        "first_values": bell_draw(splits[1], (D // BLK, N_ROW * S1, BLK, BLK), (D // 4) ** -0.5, 0.109375, ((0, 4), (1, 8))),
        "first_blocks": draw_first_blocks(jax.random.fold_in(splits[6], 71), 0),
        "second_values": bell_draw(splits[3], (F // BLK, N_COL * S2, BLK, BLK), (F // 4) ** -0.5, 0.0546875, ((0, 8), (1, 4))),
        "second_blocks": draw_second_blocks(jax.random.fold_in(splits[6], 71), 0),
        "cotangent": bell_draw(splits[5], (TOKENS, D), 1.0, 6.0, ((0, 8), (1, 4))),
    }


gelu_scale = 0.7978845608028654
gelu_cubic = 0.044715


def gelu_pair(pre_act):
    inner_arg = gelu_scale * (pre_act + gelu_cubic * pre_act * pre_act * pre_act)
    tanh_value = jnp.tanh(inner_arg)
    activated = 0.5 * pre_act * (1.0 + tanh_value)
    derivative = 0.5 * (1.0 + tanh_value) + 0.5 * pre_act * (1.0 - tanh_value * tanh_value) * gelu_scale * (1.0 + 3.0 * gelu_cubic * pre_act * pre_act)
    return activated, derivative


def spread(panels, values, blocks, out_blocks):
    row_count = panels.shape[0]
    side = values.shape[2]
    shaped = panels.reshape(row_count, values.shape[0], side)

    def add_row(row_index, running):
        source = shaped[:, row_index, :].astype(jnp.float32)
        weights = values[row_index].astype(jnp.float32)
        terms = jnp.einsum("tk,sko->tso", source, weights, precision=lax.Precision.HIGHEST)
        return running.at[:, blocks[row_index], :].add(terms)

    initial = jnp.zeros((row_count, out_blocks, side), jnp.float32)
    running = lax.fori_loop(0, values.shape[0], add_row, initial)
    return running.reshape(row_count, out_blocks * side)


def gather_back(out_grad, kept, values, blocks):
    row_count = out_grad.shape[0]
    side = values.shape[2]
    grad_shaped = out_grad.reshape(row_count, -1, side)
    kept_shaped = kept.reshape(row_count, values.shape[0], side)

    def one_row(row_index):
        picked = grad_shaped[:, blocks[row_index], :].astype(jnp.float32)
        weights = values[row_index].astype(jnp.float32)
        backward = jnp.einsum("tso,sko->tk", picked, weights, precision=lax.Precision.HIGHEST)
        source = kept_shaped[:, row_index, :].astype(jnp.float32)
        grad_blocks = jnp.einsum("tk,tso->sko", source, picked, precision=lax.Precision.HIGHEST)
        return backward, grad_blocks

    backward, grad_blocks = lax.map(one_row, jnp.arange(values.shape[0], dtype=jnp.int32))
    backward = jnp.transpose(backward, (1, 0, 2)).reshape(row_count, values.shape[0] * side)
    return backward, grad_blocks


def reference(inputs, first_values, first_blocks, second_values, second_blocks, cotangent):
    pre_act = spread(inputs, first_values, first_blocks.astype(jnp.int32), F // BLK)
    activated, derivative = gelu_pair(pre_act)
    hidden = activated.astype(jnp.bfloat16)
    outputs = spread(hidden, second_values, second_blocks.astype(jnp.int32), D // BLK).astype(jnp.bfloat16)
    hidden_grad, second_grad = gather_back(cotangent, hidden, second_values, second_blocks.astype(jnp.int32))
    pre_grad = (hidden_grad * derivative).astype(jnp.bfloat16)
    input_grad, first_grad = gather_back(pre_grad, inputs, first_values, first_blocks.astype(jnp.int32))
    return outputs, input_grad.astype(jnp.bfloat16), first_grad.astype(jnp.bfloat16), second_grad.astype(jnp.bfloat16)
```

```python
import functools

import jax
import jax.numpy as jnp
from jax import lax
from jax.experimental import pallas as pl
from jax.experimental.pallas import tpu as pltpu
from jax.sharding import PartitionSpec as P

gelu_scale = 0.7978845608028654
gelu_cubic = 0.044715

CHUNKS = 3
PARTS = 2
DELAY = 2
VMEM_BYTES = 56 * 2**20


def gelu_pair(pre_act):
    inner_arg = gelu_scale * (pre_act + gelu_cubic * pre_act * pre_act * pre_act)
    tanh_value = jnp.tanh(inner_arg)
    activated = 0.5 * pre_act * (1.0 + tanh_value)
    derivative = 0.5 * (1.0 + tanh_value) + 0.5 * pre_act * (
        1.0 - tanh_value * tanh_value
    ) * gelu_scale * (1.0 + 3.0 * gelu_cubic * pre_act * pre_act)
    return (activated, derivative)


def divisor(total, most):
    return max(size for size in range(1, most + 1) if total % size == 0)


def params():
    return pltpu.CompilerParams(
        vmem_limit_bytes=VMEM_BYTES, dimension_semantics=("arbitrary",)
    )


def groups_of(count, width):
    return [list(range(at, min(at + width, count))) for at in range(0, count, width)]


def spread(panel, values, index, out_blocks, out_groups):
    groups, rows, tokens, side = panel.shape
    slots = values.shape[1]
    total = groups * tokens
    per = divisor(rows, max(1, 48 // slots))

    def body(index_ref, panel_ref, value_ref, out_ref):
        step = pl.program_id(0)

        @pl.when(step == 0)
        def _():
            out_ref[...] = jnp.zeros_like(out_ref)

        for local in range(per):
            source = panel_ref[:, local].reshape(total, side)
            for group in groups_of(slots, 2):
                weights = jnp.concatenate([value_ref[local, s] for s in group], axis=1)
                product = jnp.dot(source, weights, preferred_element_type=jnp.float32)
                for at, s in enumerate(group):
                    block = index_ref[(step * per + local) * slots + s]
                    piece = product[:, at * side : (at + 1) * side]
                    out_ref[:, block] += piece.reshape(out_groups, total // out_groups, side)

    out_shape = (out_groups, out_blocks, total // out_groups, side)
    return pl.pallas_call(
        body,
        grid_spec=pltpu.PrefetchScalarGridSpec(
            num_scalar_prefetch=1,
            grid=(rows // per,),
            in_specs=[
                pl.BlockSpec((groups, per, tokens, side), lambda i, ref: (0, i, 0, 0)),
                pl.BlockSpec((per, slots, side, side), lambda i, ref: (i, 0, 0, 0)),
            ],
            out_specs=pl.BlockSpec(out_shape, lambda i, ref: (0, 0, 0, 0)),
        ),
        out_shape=jax.ShapeDtypeStruct(out_shape, jnp.float32),
        compiler_params=params(),
        cost_estimate=pl.CostEstimate(
            flops=8 * total * rows * slots * side * side,
            bytes_accessed=2 * values.size + 2 * panel.size + 16 * total * out_blocks * side,
            transcendentals=0,
        ),
        name="spread",
    )(index, panel, values)


def collect(panel, values, index, out_groups):
    groups, blocks, tokens, side = panel.shape
    rows, slots = values.shape[:2]
    total = groups * tokens
    per = divisor(rows, max(1, 48 // slots))

    def body(index_ref, panel_ref, value_ref, out_ref):
        step = pl.program_id(0)
        for local in range(per):
            picked = []
            for s in range(slots):
                block = index_ref[(step * per + local) * slots + s]
                picked.append(panel_ref[:, block].reshape(total, side))
            weights = jnp.concatenate([value_ref[local, s] for s in range(slots)], axis=1)
            summed = lax.dot_general(
                jnp.concatenate(picked, axis=1),
                weights,
                (((1,), (1,)), ((), ())),
                preferred_element_type=jnp.float32,
            )
            out_ref[:, local] = summed.reshape(out_groups, total // out_groups, side)

    return pl.pallas_call(
        body,
        grid_spec=pltpu.PrefetchScalarGridSpec(
            num_scalar_prefetch=1,
            grid=(rows // per,),
            in_specs=[
                pl.BlockSpec(panel.shape, lambda i, ref: (0, 0, 0, 0)),
                pl.BlockSpec((per, slots, side, side), lambda i, ref: (i, 0, 0, 0)),
            ],
            out_specs=pl.BlockSpec(
                (out_groups, per, total // out_groups, side), lambda i, ref: (0, i, 0, 0)
            ),
        ),
        out_shape=jax.ShapeDtypeStruct(
            (out_groups, rows, total // out_groups, side), jnp.float32
        ),
        compiler_params=params(),
        cost_estimate=pl.CostEstimate(
            flops=8 * total * rows * slots * side * side,
            bytes_accessed=2 * values.size + 2 * panel.size + 4 * total * rows * side,
            transcendentals=0,
        ),
        name="collect",
    )(index, panel, values)


def block_grads(lefts, rights, index, slots):
    side = lefts[0].shape[3]
    rows = lefts[0].shape[1]
    per = divisor(rows, max(1, 24 // slots))
    count = len(lefts)
    all_tokens = sum(panel.shape[0] * panel.shape[2] for panel in lefts)

    def flat(piece):
        return piece.reshape(piece.shape[0] * piece.shape[1], side)

    def body(index_ref, *refs):
        left_refs, right_refs, out_ref = refs[:count], refs[count : 2 * count], refs[-1]
        step = pl.program_id(0)
        for local in range(per):
            left = jnp.concatenate([flat(ref[:, local]) for ref in left_refs], axis=0)
            turned = left.T
            for group in groups_of(slots, 2):
                columns = []
                for s in group:
                    block = index_ref[(step * per + local) * slots + s]
                    columns.append(
                        jnp.concatenate([flat(ref[:, block]) for ref in right_refs], axis=0)
                    )
                product = jnp.dot(
                    turned,
                    jnp.concatenate(columns, axis=1),
                    preferred_element_type=jnp.float32,
                )
                for at, s in enumerate(group):
                    out_ref[local, s] = product[:, at * side : (at + 1) * side].astype(
                        out_ref.dtype
                    )

    left_specs = [
        pl.BlockSpec((p.shape[0], per, p.shape[2], side), lambda i, ref: (0, i, 0, 0))
        for p in lefts
    ]
    right_specs = [pl.BlockSpec(p.shape, lambda i, ref: (0, 0, 0, 0)) for p in rights]
    return pl.pallas_call(
        body,
        grid_spec=pltpu.PrefetchScalarGridSpec(
            num_scalar_prefetch=1,
            grid=(rows // per,),
            in_specs=left_specs + right_specs,
            out_specs=pl.BlockSpec((per, slots, side, side), lambda i, ref: (i, 0, 0, 0)),
        ),
        out_shape=jax.ShapeDtypeStruct((rows, slots, side, side), jnp.bfloat16),
        compiler_params=params(),
        cost_estimate=pl.CostEstimate(
            flops=8 * all_tokens * rows * slots * side * side,
            bytes_accessed=2 * sum(p.size for p in lefts + rights)
            + 2 * rows * slots * side * side,
            transcendentals=0,
        ),
        name="block_grads",
    )(index, *lefts, *rights)


def sum_step(position, lanes, part_blocks):
    last = None
    for lane in lanes:
        last = lane["last"]
    sample = next(iter(lanes[0]["parts"].values()))[0]
    tokens, side = sample.shape[2], sample.shape[3]
    per = divisor(part_blocks, 6)
    operands, in_specs, out_specs, out_shapes = [], [], [], []
    block = (per, tokens, side)

    def whole(j, ref):
        return (j, 0, 0)

    for which, lane in enumerate(lanes):
        if lane["received"] is not None:
            operands.append(lane["received"])
            in_specs.append(
                pl.BlockSpec(
                    block,
                    lambda j, ref, which=which: (jnp.where(ref[which] > 0, j, 0), 0, 0),
                )
            )
        for place, (array, half, part) in lane["parts"].items():
            operands.append(array)

            def at_part(j, ref, which=which, place=place, half=half, part=part):
                first = part * (part_blocks // per)
                return (half, jnp.where(ref[which] == place, first + j, first), 0, 0)

            in_specs.append(pl.BlockSpec((None,) + block, at_part))
        if lane["kind"] == "grad":
            operands.append(lane["saved"])
            in_specs.append(
                pl.BlockSpec(
                    block,
                    lambda j, ref, which=which: (jnp.where(ref[which] == last, j, 0), 0, 0),
                )
            )
        out_specs.append(pl.BlockSpec(block, whole))
        out_shapes.append(jax.ShapeDtypeStruct((part_blocks, tokens, side), jnp.bfloat16))
        if lane["kind"] == "pre":
            out_specs.append(pl.BlockSpec(block, whole))
            out_shapes.append(jax.ShapeDtypeStruct((part_blocks, tokens, side), jnp.float32))

    def body(position_ref, *refs):
        ins, outs = list(refs[: len(operands)]), list(refs[len(operands) :])
        for which, lane in enumerate(lanes):
            received = ins.pop(0) if lane["received"] is not None else None
            part_refs = {place: ins.pop(0) for place in lane["parts"]}
            saved = ins.pop(0) if lane["kind"] == "grad" else None
            out = outs.pop(0)
            kept = outs.pop(0) if lane["kind"] == "pre" else None

            for place, part_ref in part_refs.items():

                @pl.when(position_ref[which] == place)
                def _(place=place, part_ref=part_ref):
                    total = part_ref[...]
                    if place > 0:
                        total = total + received[...].astype(jnp.float32)
                    if place < last:
                        out[...] = total.astype(jnp.bfloat16)
                    elif lane["kind"] == "pre":
                        kept[...] = total
                        out[...] = gelu_pair(total)[0].astype(jnp.bfloat16)
                    else:
                        out[...] = (total * gelu_pair(saved[...])[1]).astype(jnp.bfloat16)

    made = pl.pallas_call(
        body,
        grid_spec=pltpu.PrefetchScalarGridSpec(
            num_scalar_prefetch=1,
            grid=(part_blocks // per,),
            in_specs=in_specs,
            out_specs=out_specs,
        ),
        out_shape=out_shapes,
        compiler_params=params(),
        cost_estimate=pl.CostEstimate(
            flops=20 * part_blocks * tokens * side,
            bytes_accessed=20 * part_blocks * tokens * side,
            transcendentals=0,
        ),
        name="sum_step",
    )(position, *operands)
    made = list(made)
    results = []
    for lane in lanes:
        out = made.pop(0)
        results.append((out, made.pop(0) if lane["kind"] == "pre" else None))
    return results


def pick(position, choices, part_blocks):
    tokens, side = choices[0][0][0].shape[1:]
    parts = len(choices[0])
    per = divisor(part_blocks, 8)
    steps = part_blocks // per
    operands, in_specs, owners = [], [], []
    for which, lane in enumerate(choices):
        for part, arrays in enumerate(lane):
            for place, array in enumerate(arrays):

                def at(j, ref, which=which, part=part, place=place):
                    here = (ref[which] == place) & (j // steps == part)
                    return (jnp.where(here, j % steps, jnp.where(j // steps > part, steps - 1, 0)), 0, 0)

                operands.append(array)
                in_specs.append(pl.BlockSpec((per, tokens, side), at))
                owners.append((which, part, place))

    def body(position_ref, *refs):
        j = pl.program_id(0)
        out = refs[-1]
        for ref, (which, part, place) in zip(refs[:-1], owners):

            @pl.when((position_ref[which] == place) & (j // steps == part))
            def _(ref=ref, which=which):
                out[which] = ref[...]

    shape = (len(choices), parts * part_blocks, tokens, side)
    return pl.pallas_call(
        body,
        grid_spec=pltpu.PrefetchScalarGridSpec(
            num_scalar_prefetch=1,
            grid=(parts * steps,),
            in_specs=in_specs,
            out_specs=pl.BlockSpec(
                (len(choices), per, tokens, side), lambda j, ref: (0, j, 0, 0)
            ),
        ),
        out_shape=jax.ShapeDtypeStruct(shape, jnp.bfloat16),
        compiler_params=params(),
        cost_estimate=pl.CostEstimate(
            flops=0, bytes_accessed=4 * parts * part_blocks * tokens * side * 2, transcendentals=0
        ),
        name="pick",
    )(position, *operands)


def shards(inputs, first_values, first_blocks, second_values, second_blocks, cotangent):
    n_row, n_col = lax.axis_size("row"), lax.axis_size("col")
    last = n_col - 1
    tiles, first_slots, side = first_values.shape[:3]
    hidden, second_slots = second_values.shape[:2]
    own = inputs.shape[0]
    chunks = divisor(own // 8, CHUNKS)
    parts = divisor(hidden, PARTS)
    part_blocks = hidden // parts
    rows = own // chunks

    first_index = (first_blocks - lax.axis_index("row") * hidden).reshape(-1)
    second_index = (second_blocks - lax.axis_index("col") * tiles).reshape(-1)
    place = lax.axis_index("col").astype(jnp.int32)
    position = jnp.stack([place, last - place])

    def by_block(array):
        return array.reshape(own, tiles, side).transpose(1, 0, 2)

    def gathered(array):
        return [
            lax.all_gather(array[:, c * rows : (c + 1) * rows], "row") for c in range(chunks)
        ]

    input_panels = gathered(by_block(inputs))
    grad_panels = gathered(by_block(cotangent))

    first_terms = [spread(p, first_values, first_index, hidden, 2) for p in input_panels]
    hidden_terms = [collect(p, second_values, second_index, 2) for p in grad_panels]
    terms = [(array, part) for array in first_terms + hidden_terms for part in range(parts)]
    items = len(terms)
    halves = (1, 0)

    up = [(k, k + 1) for k in range(last)]
    down = [(k + 1, k) for k in reversed(range(last))]
    sum_pairs, back_pairs = (up, down), (down, up)

    def active(pairs, step):
        return [pair for k, pair in enumerate(pairs) if 0 <= step - DELAY * k < items]

    summed = [{}, {}]
    kept = [{}, {}]
    moved = [{}, {}]
    returned = [{}, {}]
    back_start = max(items, DELAY * last + 1)
    steps = back_start + items + DELAY * (last - 1)

    for step in range(steps):
        work = {
            k: step - DELAY * k for k in range(n_col) if 0 <= step - DELAY * k < items
        }
        if work:
            lanes = []
            for which in range(2):
                kind = None
                if last in work:
                    kind = "pre" if work[last] < items // 2 else "grad"
                lanes.append(
                    {
                        "received": moved[which].get(step - DELAY),
                        "parts": {
                            k: (terms[item][0], halves[which], terms[item][1])
                            for k, item in work.items()
                        },
                        "kind": kind,
                        "saved": kept[which].get(step - items // 2),
                        "last": last,
                    }
                )
            for which, (out, pre) in enumerate(sum_step(position, lanes, part_blocks)):
                summed[which][step] = out
                kept[which][step] = pre
        for which in range(2):
            pairs = active(sum_pairs[which], step)
            if pairs:
                moved[which][step] = lax.ppermute(summed[which][step], "col", pairs)
            back = step - back_start
            pairs = active(back_pairs[which], back)
            if pairs:
                fresh = summed[which].get(back + DELAY * last) if 0 <= back < items else None
                passed = returned[which].get(step - DELAY)
                if fresh is None:
                    source = passed
                elif passed is None:
                    source = fresh
                else:
                    source = jnp.where(position[which] == last, fresh, passed)
                returned[which][step] = lax.ppermute(source, "col", pairs)

    def result_panel(chunk):
        choices = []
        for which in range(2):
            lane = []
            for part in range(parts):
                item = chunk * parts + part
                arrays = [None] * n_col
                arrays[last] = summed[which][item + DELAY * last]
                for hop in range(1, n_col):
                    arrays[last - hop] = returned[which][back_start + item + DELAY * (hop - 1)]
                lane.append(arrays)
            choices.append(lane)
        return pick(position[::-1], choices[::-1], part_blocks)

    hidden_panels = [result_panel(c) for c in range(chunks)]
    pre_panels = [result_panel(chunks + c) for c in range(chunks)]

    def scattered(panels):
        own_rows = [
            lax.psum_scatter(p, "row", scatter_dimension=0, tiled=False).astype(jnp.bfloat16)
            for p in panels
        ]
        joined = jnp.concatenate(own_rows, axis=1)
        return joined.transpose(1, 0, 2).reshape(own, tiles * side)

    outputs = scattered(
        [spread(p, second_values, second_index, tiles, n_row) for p in hidden_panels]
    )
    second_grad = block_grads(hidden_panels, grad_panels, second_index, second_slots)
    input_grad = scattered([collect(p, first_values, first_index, n_row) for p in pre_panels])
    first_grad = block_grads(input_panels, pre_panels, first_index, first_slots)
    return (outputs, input_grad, first_grad, second_grad)


def solution(mesh):
    placed = (
        P("row", "col"),
        P("col", "row", None, None),
        P("col", "row"),
        P("row", "col", None, None),
        P("row", "col"),
        P("row", "col"),
    )
    return jax.shard_map(
        shards,
        mesh=mesh,
        in_specs=placed,
        out_specs=(
            P("row", "col"),
            P("row", "col"),
            P("col", "row", None, None),
            P("row", "col", None, None),
        ),
        check_vma=False,
    )
```

```python
import functools

import jax
import jax.numpy as jnp
from jax import lax
from jax.experimental import pallas as pl
from jax.experimental.pallas import tpu as pltpu
from jax.sharding import PartitionSpec as P

gelu_scale = 0.7978845608028654
gelu_cubic = 0.044715

CHUNKS = 3
PARTS = 2
DELAY = 2
PIECES = 4
VMEM_BYTES = 64 * 2**20 - 600 * 2**10


def gelu_pair(pre_act):
    inner_arg = gelu_scale * (pre_act + gelu_cubic * pre_act * pre_act * pre_act)
    tanh_value = jnp.tanh(inner_arg)
    activated = 0.5 * pre_act * (1.0 + tanh_value)
    derivative = 0.5 * (1.0 + tanh_value) + 0.5 * pre_act * (
        1.0 - tanh_value * tanh_value
    ) * gelu_scale * (1.0 + 3.0 * gelu_cubic * pre_act * pre_act)
    return (activated, derivative)


def divisor(total, most):
    return max(size for size in range(1, most + 1) if total % size == 0)


def params():
    return pltpu.CompilerParams(
        vmem_limit_bytes=VMEM_BYTES, dimension_semantics=("arbitrary",)
    )


def groups_of(count, width):
    return [list(range(at, min(at + width, count))) for at in range(0, count, width)]


ANY = pl.BlockSpec(memory_space=pl.ANY)


def view_spec(view, blocks, index):
    array, offset, tokens = view
    assert offset % tokens == 0
    shape = (array.shape[0], blocks, tokens, array.shape[3])
    return pl.BlockSpec(shape, lambda i, *refs: (0, index(i), offset // tokens, 0))


def chosen_copies(choices, refs, target, sems):
    copies = []
    at = 0
    for half, lane in enumerate(choices):
        for part, arrays in enumerate(lane):
            blocks = arrays[0].shape[0]
            for place in range(len(arrays)):
                copies.append(
                    (
                        half,
                        place,
                        pltpu.make_async_copy(
                            refs[at],
                            target.at[half, pl.ds(part * blocks, blocks)],
                            sems.at[half, part],
                        ),
                    )
                )
                at += 1
    return copies


def fetch(copies, position_ref):
    for act in ("start", "wait"):
        for half, place, copy in copies:

            @pl.when(position_ref[half] == place)
            def _(copy=copy, act=act):
                getattr(copy, act)()


def product_kernel(name, panel, values, index, position, out_shape, out_spec, work, after, resident):
    rows, slots, side = values.shape[:3]
    per = divisor(rows, max(1, 48 // slots))
    chosen = isinstance(panel, list)
    flat = [array for lane in panel for arrays in lane for array in arrays] if chosen else []
    if chosen:
        half_tokens = flat[0].shape[1]
        all_blocks = sum(arrays[0].shape[0] for arrays in panel[0])
        panel_shape = (len(panel), all_blocks, half_tokens, side)
        panel_specs, panel_operands = [ANY] * len(flat), flat
        out_specs = [out_spec(per), ANY]
        out_shapes = [out_shape, jax.ShapeDtypeStruct(panel_shape, jnp.bfloat16)]
        scratch = [
            pltpu.VMEM(panel_shape, jnp.bfloat16),
            pltpu.SemaphoreType.DMA((len(panel), len(panel[0]))),
            pltpu.SemaphoreType.DMA(()),
        ]
    else:
        blocks = panel[0].shape[1]
        spec = view_spec(panel, blocks, lambda i: 0) if resident else view_spec(panel, per, lambda i: i)
        panel_specs, panel_operands = [spec], [panel[0]]
        out_specs, out_shapes, scratch = [out_spec(per)], [out_shape], []
    total = 2 * flat[0].shape[1] if chosen else panel[0].shape[0] * panel[2]
    last_step = rows // per - 1

    def body(index_ref, position_ref, value_ref, *refs):
        step = pl.program_id(0)
        if chosen:
            panel_refs = refs[: len(flat)]
            out_ref, kept_ref, held, sems, kept_sem = refs[len(flat) + len(after) :]
            keep = pltpu.make_async_copy(held, kept_ref, kept_sem)

            @pl.when(step == 0)
            def _():
                fetch(chosen_copies(panel, panel_refs, held, sems), position_ref)
                keep.start()

            def read(block, local):
                at = step * per + local if block is None else block
                return held[:, at].reshape(total, side)

        else:
            panel_ref, out_ref = refs[0], refs[1 + len(after)]

            def read(block, local):
                at = local if block is None else block
                return panel_ref[:, at].reshape(total, side)

        work(step, per, read, value_ref, index_ref, out_ref)
        if chosen:

            @pl.when(step == last_step)
            def _():
                keep.wait()

    made = pl.pallas_call(
        body,
        grid_spec=pltpu.PrefetchScalarGridSpec(
            num_scalar_prefetch=2,
            grid=(rows // per,),
            in_specs=[pl.BlockSpec((per, slots, side, side), lambda i, *refs: (i, 0, 0, 0))]
            + panel_specs
            + [ANY] * len(after),
            out_specs=out_specs,
            scratch_shapes=scratch,
        ),
        out_shape=out_shapes,
        compiler_params=params(),
        cost_estimate=pl.CostEstimate(flops=2**20, bytes_accessed=2**20, transcendentals=0),
        name=name,
    )(index, position, values, *panel_operands, *after)
    return made if chosen else made[0]


def spread(panel, values, index, position, out_blocks, out_groups, total, after=()):
    slots, side = values.shape[1:3]
    shape = (out_groups, out_blocks, total // out_groups, side)

    def work(step, per, read, value_ref, index_ref, out_ref):
        @pl.when(step == 0)
        def _():
            out_ref[...] = jnp.zeros_like(out_ref)

        for local in range(per):
            source = read(None, local)
            for group in groups_of(slots, 2):
                weights = jnp.concatenate([value_ref[local, s] for s in group], axis=1)
                product = jnp.dot(source, weights, preferred_element_type=jnp.float32)
                for at, s in enumerate(group):
                    block = index_ref[(step * per + local) * slots + s]
                    piece = product[:, at * side : (at + 1) * side]
                    out_ref[:, block] += piece.reshape(out_groups, total // out_groups, side)

    return product_kernel(
        "spread",
        panel,
        values,
        index,
        position,
        jax.ShapeDtypeStruct(shape, jnp.float32),
        lambda per: pl.BlockSpec(shape, lambda i, *refs: (0, 0, 0, 0)),
        work,
        list(after),
        False,
    )


def collect(panel, values, index, position, out_groups, total, after=()):
    rows, slots, side = values.shape[:3]
    tokens = total // out_groups

    def work(step, per, read, value_ref, index_ref, out_ref):
        for local in range(per):
            picked = [
                read(index_ref[(step * per + local) * slots + s], local) for s in range(slots)
            ]
            weights = jnp.concatenate([value_ref[local, s] for s in range(slots)], axis=1)
            summed = lax.dot_general(
                jnp.concatenate(picked, axis=1),
                weights,
                (((1,), (1,)), ((), ())),
                preferred_element_type=jnp.float32,
            )
            out_ref[:, local] = summed.reshape(out_groups, tokens, side)

    return product_kernel(
        "collect",
        panel,
        values,
        index,
        position,
        jax.ShapeDtypeStruct((out_groups, rows, tokens, side), jnp.float32),
        lambda per: pl.BlockSpec((out_groups, per, tokens, side), lambda i, *refs: (0, i, 0, 0)),
        work,
        list(after),
        True,
    )


def block_grads(lefts, rights, index, slots, after=()):
    side = lefts[0][0].shape[3]
    rows = lefts[0][0].shape[1]
    per = divisor(rows, max(1, 24 // slots))
    count = len(lefts)

    def flat(piece):
        return piece.reshape(piece.shape[0] * piece.shape[1], side)

    def body(index_ref, *refs):
        left_refs, right_refs, out_ref = refs[:count], refs[count : 2 * count], refs[-1]
        step = pl.program_id(0)
        for local in range(per):
            left = jnp.concatenate([flat(ref[:, local]) for ref in left_refs], axis=0)
            turned = left.T
            for group in groups_of(slots, 2):
                columns = []
                for s in group:
                    block = index_ref[(step * per + local) * slots + s]
                    columns.append(
                        jnp.concatenate([flat(ref[:, block]) for ref in right_refs], axis=0)
                    )
                product = jnp.dot(
                    turned,
                    jnp.concatenate(columns, axis=1),
                    preferred_element_type=jnp.float32,
                )
                for at, s in enumerate(group):
                    out_ref[local, s] = product[:, at * side : (at + 1) * side].astype(
                        out_ref.dtype
                    )

    left_specs = [view_spec(view, per, lambda i: i) for view in lefts]
    right_specs = [view_spec(view, view[0].shape[1], lambda i: 0) for view in rights]
    return pl.pallas_call(
        body,
        grid_spec=pltpu.PrefetchScalarGridSpec(
            num_scalar_prefetch=1,
            grid=(rows // per,),
            in_specs=left_specs + right_specs + [ANY] * len(after),
            out_specs=pl.BlockSpec((per, slots, side, side), lambda i, *refs: (i, 0, 0, 0)),
        ),
        out_shape=jax.ShapeDtypeStruct((rows, slots, side, side), jnp.bfloat16),
        compiler_params=params(),
        cost_estimate=pl.CostEstimate(flops=2**20, bytes_accessed=2**20, transcendentals=0),
        name="block_grads",
    )(index, *[v[0] for v in lefts], *[v[0] for v in rights], *after)


def step_kernel(position, sums, passes, last, rows, after):
    side = 128
    size = rows // PIECES
    operands, out_shapes = [], []

    def operand(array):
        operands.append(array)
        return len(operands) - 1

    def result(dtype):
        out_shapes.append(jax.ShapeDtypeStruct((rows, side), dtype))
        return len(out_shapes) - 1

    plan = []
    for lane in sums:
        kind = lane["kind"]
        plan.append(
            {
                "received": None if lane["received"] is None else operand(lane["received"]),
                "parts": {k: (operand(a), half, part) for k, (a, half, part) in lane["parts"].items()},
                "saved": operand(lane["saved"]) if kind == "grad" else None,
                "kind": kind,
                "out": result(jnp.bfloat16),
                "kept": result(jnp.float32) if kind == "pre" else None,
            }
        )
    pass_plan = [
        (operand(fresh), operand(passed), result(jnp.bfloat16)) for fresh, passed in passes
    ]
    n_in = len(operands)
    scratch = []
    if plan:
        scratch = [
            pltpu.VMEM((2, rows, side), jnp.bfloat16),
            pltpu.VMEM((2, rows, side), jnp.float32),
            pltpu.VMEM((2, rows, side), jnp.float32),
            pltpu.VMEM((2, rows, side), jnp.bfloat16),
            pltpu.SemaphoreType.DMA((2, 3, PIECES)),
            pltpu.SemaphoreType.DMA((2, 2, PIECES)),
        ]
    scratch.append(pltpu.SemaphoreType.DMA((2,)))

    def body(position_ref, *refs):
        ins = refs[:n_in]
        outs = refs[n_in + len(after) : n_in + len(after) + len(out_shapes)]
        held = refs[n_in + len(after) + len(out_shapes) :]
        pass_sem = held[-1]

        def on_pass(act):
            for which, (fresh, passed, out) in enumerate(pass_plan):
                at_last = position_ref[which] == last
                for here, source in ((at_last, fresh), (jnp.logical_not(at_last), passed)):

                    @pl.when(here)
                    def _(which=which, source=source, out=out):
                        copy = pltpu.make_async_copy(ins[source], outs[out], pass_sem.at[which])
                        getattr(copy, act)()

        if plan:
            arrived, terms, third, ready, load_sem, store_sem = held[:-1]

            def loads(which, lane, place, piece):
                span = pl.ds(piece * size, size)
                array, half, part = lane["parts"][place]
                own = pl.ds(part * rows + piece * size, size)
                copies = [
                    pltpu.make_async_copy(
                        ins[array].at[half, own], terms.at[which, span], load_sem.at[which, 0, piece]
                    )
                ]
                if place > 0:
                    copies.append(
                        pltpu.make_async_copy(
                            ins[lane["received"]].at[span],
                            arrived.at[which, span],
                            load_sem.at[which, 1, piece],
                        )
                    )
                if place == last and lane["kind"] == "grad":
                    copies.append(
                        pltpu.make_async_copy(
                            ins[lane["saved"]].at[span],
                            third.at[which, span],
                            load_sem.at[which, 2, piece],
                        )
                    )
                return copies

            def stores(which, lane, place, piece):
                span = pl.ds(piece * size, size)
                copies = [
                    pltpu.make_async_copy(
                        ready.at[which, span], outs[lane["out"]].at[span], store_sem.at[which, 0, piece]
                    )
                ]
                if place == last and lane["kind"] == "pre":
                    copies.append(
                        pltpu.make_async_copy(
                            third.at[which, span],
                            outs[lane["kept"]].at[span],
                            store_sem.at[which, 1, piece],
                        )
                    )
                return copies

            def each(act):
                for which, lane in enumerate(plan):
                    for place in lane["parts"]:

                        @pl.when(position_ref[which] == place)
                        def _(which=which, lane=lane, place=place):
                            act(which, lane, place)

            def start_all(which, lane, place):
                for piece in range(PIECES):
                    for copy in loads(which, lane, place, piece):
                        copy.start()

            def add_all(which, lane, place):
                for piece in range(PIECES):
                    for copy in loads(which, lane, place, piece):
                        copy.wait()
                    span = pl.ds(piece * size, size)
                    total = terms[which, span]
                    if place > 0:
                        total = total + arrived[which, span].astype(jnp.float32)
                    if place == last and lane["kind"] == "pre":
                        third[which, span] = total
                        total = gelu_pair(total)[0]
                    elif place == last:
                        total = total * gelu_pair(third[which, span])[1]
                    ready[which, span] = total.astype(jnp.bfloat16)
                    for copy in stores(which, lane, place, piece):
                        copy.start()

            def wait_all(which, lane, place):
                for piece in range(PIECES):
                    for copy in stores(which, lane, place, piece):
                        copy.wait()

            each(start_all)
            on_pass("start")
            each(add_all)
            each(wait_all)
        else:
            on_pass("start")
        on_pass("wait")

    made = pl.pallas_call(
        body,
        grid_spec=pltpu.PrefetchScalarGridSpec(
            num_scalar_prefetch=1,
            grid=(1,),
            in_specs=[ANY] * (n_in + len(after)),
            out_specs=[ANY] * len(out_shapes),
            scratch_shapes=scratch,
        ),
        out_shape=out_shapes,
        compiler_params=params(),
        cost_estimate=pl.CostEstimate(flops=2**20, bytes_accessed=2**20, transcendentals=0),
        name="col_step",
    )(position, *operands, *after)
    sent = [made[lane["out"]] for lane in plan]
    kept = [None if lane["kept"] is None else made[lane["kept"]] for lane in plan]
    return sent, kept, [made[out] for _, _, out in pass_plan]


def link_order(items, last):
    sums, results, slot, sum_turn = [], [], 0, True
    while len(results) < items:
        more_sums = len(sums) < items
        can_pass = len(results) < len(sums) and slot > sums[len(results)] + DELAY * last
        if more_sums and (len(sums) < items // 2 or sum_turn or not can_pass):
            sums.append(slot)
            sum_turn = False
        elif can_pass:
            results.append(slot)
            sum_turn = True
        slot += 1
    return sums, results


def shards(inputs, first_values, first_blocks, second_values, second_blocks, cotangent):
    n_row, n_col = lax.axis_size("row"), lax.axis_size("col")
    last = n_col - 1
    tiles, first_slots, side = first_values.shape[:3]
    hidden, second_slots = second_values.shape[:2]
    own = inputs.shape[0]
    chunks = divisor(own // 16, CHUNKS)
    parts = divisor(hidden, PARTS)
    part_blocks = hidden // parts
    rows = own // chunks
    total = rows * n_row
    item_rows = part_blocks * total // 2

    first_index = (first_blocks - lax.axis_index("row") * hidden).reshape(-1)
    second_index = (second_blocks - lax.axis_index("col") * tiles).reshape(-1)
    place = lax.axis_index("col").astype(jnp.int32)
    position = jnp.stack([place, last - place])
    result_place = jnp.stack([place, place])

    def by_block(array):
        return array.reshape(own, tiles, side).transpose(1, 0, 2)

    first = by_block(inputs)
    opening = lax.all_gather(first[:, :rows], "row")
    input_views = [(opening, 0, rows)]
    if chunks > 1:
        others = lax.all_gather(first[:, rows:], "row")
        input_views += [(others, at * rows, rows) for at in range(chunks - 1)]
    gathered = lax.all_gather(by_block(cotangent), "row")
    grad_views = [(gathered, at * rows, rows) for at in range(chunks)]

    items = 2 * chunks * parts
    sum_slots, result_slots = link_order(items, last)
    steps = result_slots[-1] + DELAY * (last - 1) + 1

    terms = {}
    panels = {}
    products = {}
    moved = [{}, {}]
    summed = [{}, {}]
    kept = [{}, {}]
    returned = [{}, {}]
    halves = (1, 0)
    up = [(k, k + 1) for k in range(last)]
    down = [(k + 1, k) for k in reversed(range(last))]
    sum_pairs, back_pairs = (up, down), (down, up)

    def sum_item(step, k):
        slot = step - DELAY * k
        return sum_slots.index(slot) if slot in sum_slots else None

    def result_item(step, k):
        slot = step - DELAY * k
        return result_slots.index(slot) if slot in result_slots else None

    def make_terms(chunk, after):
        if chunk < chunks:
            made = spread(
                input_views[chunk], first_values, first_index, position, hidden, 2, total, after
            )
        else:
            made = collect(
                grad_views[chunk - chunks], second_values, second_index, position, 2, total, after
            )
        terms[chunk] = made.reshape(2, hidden * total // 2, side)
        return made

    def make_product(chunk, after):
        choices = []
        for half in range(2):
            which = halves.index(half)
            lane = []
            for part in range(parts):
                item = chunk * parts + part
                arrays = {last: summed[which][sum_slots[item] + DELAY * last]}
                for hop in range(1, n_col):
                    arrays[last - hop] = returned[which][result_slots[item] + DELAY * (hop - 1)]
                ordered = [arrays[k if which == 0 else last - k] for k in range(n_col)]
                lane.append([a.reshape(part_blocks, total // 2, side) for a in ordered])
            choices.append(lane)
        if chunk < chunks:
            made = spread(
                choices, second_values, second_index, result_place, tiles, n_row, total, after
            )
        else:
            made = collect(choices, first_values, first_index, result_place, n_row, total, after)
        products[chunk], panel = made
        panels[chunk] = (panel, 0, total // 2)
        return made[0]

    def make_second_grad(after):
        products["second"] = block_grads(
            [panels[c] for c in range(chunks)], grad_views, second_index, second_slots, after
        )
        return products["second"]

    queue = {}
    for chunk in range(1, 2 * chunks):
        queue.setdefault(sum_slots[chunk * parts] - 1, []).append(
            functools.partial(make_terms, chunk)
        )
    for chunk in range(2 * chunks):
        ready = result_slots[(chunk + 1) * parts - 1] + DELAY * last
        queue.setdefault(min(ready, steps), []).append(functools.partial(make_product, chunk))
        if chunk == chunks - 1:
            queue.setdefault(min(ready + 1, steps), []).append(make_second_grad)

    before = [make_terms(0, ())]
    mark = None
    for step in range(steps):
        work = {k: sum_item(step, k) for k in range(n_col) if sum_item(step, k) is not None}
        sums, passes = [], []
        if work:
            for which in range(2):
                kind = None
                if last in work:
                    kind = "pre" if work[last] < items // 2 else "grad"
                sums.append(
                    {
                        "received": moved[which].get(step - DELAY),
                        "parts": {
                            k: (terms[item // parts], halves[which], item % parts)
                            for k, item in work.items()
                        },
                        "kind": kind,
                        "saved": kept[which].get(work[last] - items // 2) if kind else None,
                    }
                )
        back = {k: result_item(step, k) for k in range(last) if result_item(step, k) is not None}
        sources = [None, None]
        if back:
            for which in range(2):
                if 0 in back:
                    sources[which] = summed[which][sum_slots[back[0]] + DELAY * last]
                if len(back) > (0 in back):
                    passed = returned[which][step - DELAY]
                    if 0 in back:
                        passes.append((sources[which], passed))
                    sources[which] = passed
        if sums or passes:
            out, pre, passed = step_kernel(position, sums, passes, last, item_rows, before)
            before = []
            mark = (out + passed)[0]
            for which in range(2):
                if sums:
                    summed[which][step] = out[which]
                    if pre[which] is not None:
                        kept[which][work[last]] = pre[which]
                if passes:
                    sources[which] = passed[which]
        for which in range(2):
            pairs = [sum_pairs[which][k] for k in work if k < last]
            if pairs:
                moved[which][step] = lax.ppermute(summed[which][step], "col", pairs)
            pairs = [back_pairs[which][k] for k in back]
            if pairs:
                returned[which][step] = lax.ppermute(sources[which], "col", pairs)
        for make in queue.get(step, []):
            before.append(make([mark]))
    for make in queue.get(steps, []):
        before = [make(before[-1:])]

    def scattered(chunk):
        array = products[chunk]
        if chunk >= chunks and n_row % 2 == 0:
            core = lax.axis_index("row") % 2
            pairs = array.reshape((n_row // 2, 2) + array.shape[1:])
            other = lax.ppermute(
                lax.dynamic_index_in_dim(pairs, 1 - core, 1, keepdims=False),
                "row",
                [(r, r ^ 1) for r in range(n_row)],
            )
            array = other + lax.dynamic_index_in_dim(pairs, core, 1, keepdims=False)
            groups = [list(range(c, n_row, 2)) for c in range(2)]
        else:
            groups = None
        return lax.psum_scatter(
            array, "row", scatter_dimension=0, axis_index_groups=groups, tiled=False
        ).astype(jnp.bfloat16)

    def joined(first_chunk):
        own_rows = [scattered(first_chunk + c) for c in range(chunks)]
        return jnp.concatenate(own_rows, axis=1).transpose(1, 0, 2).reshape(own, tiles * side)

    outputs = joined(0)
    input_grad = joined(chunks)
    first_grad = block_grads(
        input_views, [panels[chunks + c] for c in range(chunks)], first_index, first_slots, before
    )
    return (outputs, input_grad, first_grad, products["second"])


def solution(mesh):
    placed = (
        P("row", "col"),
        P("col", "row", None, None),
        P("col", "row"),
        P("row", "col", None, None),
        P("row", "col"),
        P("row", "col"),
    )
    return jax.shard_map(
        shards,
        mesh=mesh,
        in_specs=placed,
        out_specs=(
            P("row", "col"),
            P("row", "col"),
            P("col", "row", None, None),
            P("row", "col", None, None),
        ),
        check_vma=False,
    )
```

```python
import functools

import jax
import jax.numpy as jnp
from jax import lax
from jax.experimental import pallas as pl
from jax.experimental.pallas import tpu as pltpu
from jax.sharding import PartitionSpec as P

gelu_scale = 0.7978845608028654
gelu_cubic = 0.044715

CHUNKS = 3
PARTS = 2
DELAY = 2
PIECES = 4
VMEM_BYTES = 64 * 2**20 - 600 * 2**10


def gelu_pair(pre_act):
    inner_arg = gelu_scale * (pre_act + gelu_cubic * pre_act * pre_act * pre_act)
    tanh_value = jnp.tanh(inner_arg)
    activated = 0.5 * pre_act * (1.0 + tanh_value)
    derivative = 0.5 * (1.0 + tanh_value) + 0.5 * pre_act * (
        1.0 - tanh_value * tanh_value
    ) * gelu_scale * (1.0 + 3.0 * gelu_cubic * pre_act * pre_act)
    return (activated, derivative)


def divisor(total, most):
    return max(size for size in range(1, most + 1) if total % size == 0)


def params():
    return pltpu.CompilerParams(
        vmem_limit_bytes=VMEM_BYTES, dimension_semantics=("arbitrary",)
    )


def groups_of(count, width):
    return [list(range(at, min(at + width, count))) for at in range(0, count, width)]


ANY = pl.BlockSpec(memory_space=pl.ANY)


def view_spec(view, blocks, index):
    array, offset, tokens = view
    assert offset % tokens == 0
    shape = (array.shape[0], blocks, tokens, array.shape[3])
    return pl.BlockSpec(shape, lambda i, *refs: (0, index(i), offset // tokens, 0))


def chosen_copies(choices, refs, target, sems):
    copies = []
    at = 0
    for half, lane in enumerate(choices):
        for part, arrays in enumerate(lane):
            blocks = arrays[0].shape[0]
            for place in range(len(arrays)):
                copies.append(
                    (
                        half,
                        place,
                        pltpu.make_async_copy(
                            refs[at],
                            target.at[half, pl.ds(part * blocks, blocks)],
                            sems.at[half, part],
                        ),
                    )
                )
                at += 1
    return copies


def fetch(copies, position_ref):
    for act in ("start", "wait"):
        for half, place, copy in copies:

            @pl.when(position_ref[half] == place)
            def _(copy=copy, act=act):
                getattr(copy, act)()


def product_kernel(
    name, panel, values, index, position, out_shape, out_spec, work, after, resident, sums=None
):
    rows, slots, side = values.shape[:3]
    per = divisor(rows, max(1, 48 // slots))
    chosen = isinstance(panel, list)
    flat = [array for lane in panel for arrays in lane for array in arrays] if chosen else []
    if chosen:
        half_tokens = flat[0].shape[1]
        all_blocks = sum(arrays[0].shape[0] for arrays in panel[0])
        panel_shape = (len(panel), all_blocks, half_tokens, side)
        panel_specs, panel_operands = [ANY] * len(flat), flat
        out_specs = [out_spec(per), ANY]
        out_shapes = [out_shape, jax.ShapeDtypeStruct(panel_shape, jnp.bfloat16)]
        scratch = [
            pltpu.VMEM(panel_shape, jnp.bfloat16),
            pltpu.SemaphoreType.DMA((len(panel), len(panel[0]))),
            pltpu.SemaphoreType.DMA(()),
        ]
    else:
        blocks = panel[0].shape[1]
        spec = view_spec(panel, blocks, lambda i: 0) if resident else view_spec(panel, per, lambda i: i)
        panel_specs, panel_operands = [spec], [panel[0]]
        out_specs, out_shapes, scratch = [out_spec(per)], [out_shape], []
    if sums is not None:
        scratch.append(pltpu.VMEM(sums, jnp.float32))
    total = 2 * flat[0].shape[1] if chosen else panel[0].shape[0] * panel[2]
    last_step = rows // per - 1

    def body(index_ref, position_ref, value_ref, *refs):
        step = pl.program_id(0)
        total_ref = None
        if sums is not None:
            refs, total_ref = refs[:-1], refs[-1]
        if chosen:
            panel_refs = refs[: len(flat)]
            out_ref, kept_ref, held, sems, kept_sem = refs[len(flat) + len(after) :]
            keep = pltpu.make_async_copy(held, kept_ref, kept_sem)

            @pl.when(step == 0)
            def _():
                fetch(chosen_copies(panel, panel_refs, held, sems), position_ref)
                keep.start()

            def read(block, local):
                at = step * per + local if block is None else block
                return held[:, at].reshape(total, side)

        else:
            panel_ref, out_ref = refs[0], refs[1 + len(after)]

            def read(block, local):
                at = local if block is None else block
                return panel_ref[:, at].reshape(total, side)

        work(step, per, read, value_ref, index_ref, out_ref, total_ref)
        if chosen:

            @pl.when(step == last_step)
            def _():
                keep.wait()

    made = pl.pallas_call(
        body,
        grid_spec=pltpu.PrefetchScalarGridSpec(
            num_scalar_prefetch=2,
            grid=(rows // per,),
            in_specs=[pl.BlockSpec((per, slots, side, side), lambda i, *refs: (i, 0, 0, 0))]
            + panel_specs
            + [ANY] * len(after),
            out_specs=out_specs,
            scratch_shapes=scratch,
        ),
        out_shape=out_shapes,
        compiler_params=params(),
        cost_estimate=pl.CostEstimate(flops=2**20, bytes_accessed=2**20, transcendentals=0),
        name=name,
    )(index, position, values, *panel_operands, *after)
    return made if chosen else made[0]


def spread(panel, values, index, position, out_blocks, out_groups, total, dtype, after=()):
    rows, slots, side = values.shape[:3]
    narrow = dtype != jnp.float32
    shape = (out_groups, out_blocks, total // out_groups, side)

    def work(step, per, read, value_ref, index_ref, out_ref, total_ref):
        total_ref = total_ref if narrow else out_ref

        @pl.when(step == 0)
        def _():
            total_ref[...] = jnp.zeros_like(total_ref)

        for local in range(per):
            source = read(None, local)
            for group in groups_of(slots, 2):
                weights = jnp.concatenate([value_ref[local, s] for s in group], axis=1)
                product = jnp.dot(source, weights, preferred_element_type=jnp.float32)
                for at, s in enumerate(group):
                    block = index_ref[(step * per + local) * slots + s]
                    piece = product[:, at * side : (at + 1) * side]
                    total_ref[:, block] += piece.reshape(out_groups, total // out_groups, side)

        if narrow:

            @pl.when(step == rows // per - 1)
            def _():
                for block in range(out_blocks):
                    out_ref[:, block] = total_ref[:, block].astype(dtype)

    return product_kernel(
        "spread",
        panel,
        values,
        index,
        position,
        jax.ShapeDtypeStruct(shape, dtype),
        lambda per: pl.BlockSpec(shape, lambda i, *refs: (0, 0, 0, 0)),
        work,
        list(after),
        False,
        shape if narrow else None,
    )


def collect(panel, values, index, position, out_groups, total, dtype, after=()):
    rows, slots, side = values.shape[:3]
    tokens = total // out_groups

    def work(step, per, read, value_ref, index_ref, out_ref, total_ref):
        for local in range(per):
            picked = [
                read(index_ref[(step * per + local) * slots + s], local) for s in range(slots)
            ]
            weights = jnp.concatenate([value_ref[local, s] for s in range(slots)], axis=1)
            summed = lax.dot_general(
                jnp.concatenate(picked, axis=1),
                weights,
                (((1,), (1,)), ((), ())),
                preferred_element_type=jnp.float32,
            )
            out_ref[:, local] = summed.reshape(out_groups, tokens, side).astype(dtype)

    return product_kernel(
        "collect",
        panel,
        values,
        index,
        position,
        jax.ShapeDtypeStruct((out_groups, rows, tokens, side), dtype),
        lambda per: pl.BlockSpec((out_groups, per, tokens, side), lambda i, *refs: (0, i, 0, 0)),
        work,
        list(after),
        True,
    )


def block_grads(lefts, rights, index, slots, after=()):
    side = lefts[0][0].shape[3]
    rows = lefts[0][0].shape[1]
    per = divisor(rows, max(1, 24 // slots))
    count = len(lefts)

    def flat(piece):
        return piece.reshape(piece.shape[0] * piece.shape[1], side)

    def body(index_ref, *refs):
        left_refs, right_refs, out_ref = refs[:count], refs[count : 2 * count], refs[-1]
        step = pl.program_id(0)
        for local in range(per):
            left = jnp.concatenate([flat(ref[:, local]) for ref in left_refs], axis=0)
            turned = left.T
            for group in groups_of(slots, 2):
                columns = []
                for s in group:
                    block = index_ref[(step * per + local) * slots + s]
                    columns.append(
                        jnp.concatenate([flat(ref[:, block]) for ref in right_refs], axis=0)
                    )
                product = jnp.dot(
                    turned,
                    jnp.concatenate(columns, axis=1),
                    preferred_element_type=jnp.float32,
                )
                for at, s in enumerate(group):
                    out_ref[local, s] = product[:, at * side : (at + 1) * side].astype(
                        out_ref.dtype
                    )

    left_specs = [view_spec(view, per, lambda i: i) for view in lefts]
    right_specs = [view_spec(view, view[0].shape[1], lambda i: 0) for view in rights]
    return pl.pallas_call(
        body,
        grid_spec=pltpu.PrefetchScalarGridSpec(
            num_scalar_prefetch=1,
            grid=(rows // per,),
            in_specs=left_specs + right_specs + [ANY] * len(after),
            out_specs=pl.BlockSpec((per, slots, side, side), lambda i, *refs: (i, 0, 0, 0)),
        ),
        out_shape=jax.ShapeDtypeStruct((rows, slots, side, side), jnp.bfloat16),
        compiler_params=params(),
        cost_estimate=pl.CostEstimate(flops=2**20, bytes_accessed=2**20, transcendentals=0),
        name="block_grads",
    )(index, *[v[0] for v in lefts], *[v[0] for v in rights], *after)


def col_step(position, lanes, last, rows, after):
    side = 128
    size = rows // PIECES
    operands, out_shapes, plan = [], [], []

    def operand(array):
        if array is None:
            return None
        operands.append(array)
        return len(operands) - 1

    def result(dtype):
        out_shapes.append(jax.ShapeDtypeStruct((rows, side), dtype))
        return len(out_shapes) - 1

    for lane in lanes:
        jobs = {}
        for place, job in lane["jobs"].items():
            jobs[place] = (job[0],) if len(job) == 1 else (job[0], operand(job[1])) + job[2:]
        plan.append(
            {
                "jobs": jobs,
                "kind": lane["kind"],
                "arrived": operand(lane["arrived"]),
                "saved": operand(lane["saved"]) if lane["kind"] == "grad" else None,
                "out": result(jnp.bfloat16),
                "kept": result(jnp.float32) if lane["kind"] == "pre" else None,
            }
        )
    n_in = len(operands)
    n_out = len(out_shapes)

    def body(position_ref, *refs):
        ins, outs = refs[:n_in], refs[n_in + len(after) : n_in + len(after) + n_out]
        arrived, terms, third, ready, load_sem, store_sem = refs[n_in + len(after) + n_out :]

        def loads(which, lane, place, piece):
            span = pl.ds(piece * size, size)
            job = lane["jobs"][place]

            def load(source, target, kind):
                return pltpu.make_async_copy(
                    source, target.at[which, span], load_sem.at[which, kind, piece]
                )

            if job[0] == "fresh":
                return [load(ins[job[1]].at[span], ready, 0)]
            if job[0] == "on":
                return [load(ins[lane["arrived"]].at[span], ready, 0)]
            array, half, part = job[1:]
            own = pl.ds(part * rows + piece * size, size)
            copies = [load(ins[array].at[half, own], terms, 0)]
            if place > 0:
                copies.append(load(ins[lane["arrived"]].at[span], arrived, 1))
            if place == last and lane["kind"] == "grad":
                copies.append(load(ins[lane["saved"]].at[span], third, 2))
            return copies

        def stores(which, lane, place, piece):
            span = pl.ds(piece * size, size)
            copies = [
                pltpu.make_async_copy(
                    ready.at[which, span], outs[lane["out"]].at[span], store_sem.at[which, 0, piece]
                )
            ]
            if place == last and lane["kind"] == "pre":
                copies.append(
                    pltpu.make_async_copy(
                        third.at[which, span],
                        outs[lane["kept"]].at[span],
                        store_sem.at[which, 1, piece],
                    )
                )
            return copies

        def each(act):
            for which, lane in enumerate(plan):
                for place in lane["jobs"]:

                    @pl.when(position_ref[which] == place)
                    def _(which=which, lane=lane, place=place):
                        act(which, lane, place)

        def start_all(which, lane, place):
            for piece in range(PIECES):
                for copy in loads(which, lane, place, piece):
                    copy.start()

        def work_all(which, lane, place):
            for piece in range(PIECES):
                for copy in loads(which, lane, place, piece):
                    copy.wait()
                span = pl.ds(piece * size, size)
                if lane["jobs"][place][0] == "sum":
                    total = terms[which, span]
                    if place > 0:
                        total = total + arrived[which, span].astype(jnp.float32)
                    if place == last and lane["kind"] == "pre":
                        third[which, span] = total
                        total = gelu_pair(total)[0]
                    elif place == last:
                        total = total * gelu_pair(third[which, span])[1]
                    ready[which, span] = total.astype(jnp.bfloat16)
                for copy in stores(which, lane, place, piece):
                    copy.start()

        def wait_all(which, lane, place):
            for piece in range(PIECES):
                for copy in stores(which, lane, place, piece):
                    copy.wait()

        each(start_all)
        each(work_all)
        each(wait_all)

    made = pl.pallas_call(
        body,
        grid_spec=pltpu.PrefetchScalarGridSpec(
            num_scalar_prefetch=1,
            grid=(1,),
            in_specs=[ANY] * (n_in + len(after)),
            out_specs=[ANY] * n_out,
            scratch_shapes=[
                pltpu.VMEM((2, rows, side), jnp.bfloat16),
                pltpu.VMEM((2, rows, side), jnp.float32),
                pltpu.VMEM((2, rows, side), jnp.float32),
                pltpu.VMEM((2, rows, side), jnp.bfloat16),
                pltpu.SemaphoreType.DMA((2, 3, PIECES)),
                pltpu.SemaphoreType.DMA((2, 2, PIECES)),
            ],
        ),
        out_shape=out_shapes,
        compiler_params=params(),
        cost_estimate=pl.CostEstimate(flops=2**20, bytes_accessed=2**20, transcendentals=0),
        name="col_step",
    )(position, *operands, *after)
    return [
        (made[lane["out"]], None if lane["kept"] is None else made[lane["kept"]]) for lane in plan
    ]


def in_order(arrays, after):
    def body(*refs):
        pass

    return pl.pallas_call(
        body,
        in_specs=[ANY] * (len(arrays) + len(after)),
        out_specs=[ANY] * len(arrays),
        out_shape=[jax.ShapeDtypeStruct(a.shape, a.dtype) for a in arrays],
        input_output_aliases={k: k for k in range(len(arrays))},
        cost_estimate=pl.CostEstimate(flops=1024, bytes_accessed=1024, transcendentals=0),
        compiler_params=pltpu.CompilerParams(vmem_limit_bytes=VMEM_BYTES),
        name="in_order",
    )(*arrays, *after)


def link_order(items, last):
    sums, results, slot, sum_turn = [], [], 0, True
    while len(results) < items:
        more_sums = len(sums) < items
        can_pass = len(results) < len(sums) and slot > sums[len(results)] + DELAY * last
        if more_sums and (len(sums) < items // 2 or sum_turn or not can_pass):
            sums.append(slot)
            sum_turn = False
        elif can_pass:
            results.append(slot)
            sum_turn = True
        slot += 1
    return sums, results


def shards(inputs, first_values, first_blocks, second_values, second_blocks, cotangent):
    n_row, n_col = lax.axis_size("row"), lax.axis_size("col")
    last = n_col - 1
    tiles, first_slots, side = first_values.shape[:3]
    hidden, second_slots = second_values.shape[:2]
    own = inputs.shape[0]
    chunks = divisor(own // 16, CHUNKS)
    parts = divisor(hidden, PARTS)
    part_blocks = hidden // parts
    rows = own // chunks
    total = rows * n_row
    item_rows = part_blocks * total // 2

    first_index = (first_blocks - lax.axis_index("row") * hidden).reshape(-1)
    second_index = (second_blocks - lax.axis_index("col") * tiles).reshape(-1)
    place = lax.axis_index("col").astype(jnp.int32)
    position = jnp.stack([place, last - place])
    result_place = jnp.stack([place, place])

    def by_block(array):
        return array.reshape(own, tiles, side).transpose(1, 0, 2)

    first = by_block(inputs)
    opening = lax.all_gather(first[:, :rows], "row")
    input_views = [(opening, 0, rows)]
    if chunks > 1:
        others = lax.all_gather(first[:, rows:], "row")
        input_views += [(others, at * rows, rows) for at in range(chunks - 1)]
    gathered = lax.all_gather(by_block(cotangent), "row")
    grad_views = [(gathered, at * rows, rows) for at in range(chunks)]

    items = 2 * chunks * parts
    sum_slots, result_slots = link_order(items, last)
    steps = result_slots[-1] + DELAY * (last - 1) + 1

    terms = {}
    panels = {}
    products = {}
    made = [{}, {}]
    kept = [{}, {}]
    arrived = [{}, {}]
    halves = (1, 0)
    up = [(k, k + 1) for k in range(last)]
    down = [(last - k, last - k - 1) for k in range(last)]

    def job(direction, step, k):
        slot = step - DELAY * k
        if slot in sum_slots:
            item = sum_slots.index(slot)
            return ("sum", terms[item // parts], halves[direction], item % parts)
        if slot in result_slots and k < last:
            item = result_slots.index(slot)
            if k > 0:
                return ("on",)
            return ("fresh", made[1 - direction][sum_slots[item] + DELAY * last])
        return None

    def make_terms(chunk, after):
        if chunk < chunks:
            result = spread(
                input_views[chunk], first_values, first_index, position, hidden, 2, total,
                jnp.float32, after,
            )
        else:
            result = collect(
                grad_views[chunk - chunks], second_values, second_index, position, 2, total,
                jnp.float32, after,
            )
        terms[chunk] = result.reshape(2, hidden * total // 2, side)
        return result

    def make_product(chunk, after):
        choices = []
        for half in range(2):
            lane = halves.index(half)
            pieces = []
            for part in range(parts):
                item = chunk * parts + part
                arrays = [made[lane][sum_slots[item] + DELAY * last]] + [
                    arrived[1 - lane][result_slots[item] + DELAY * (hop - 1)]
                    for hop in range(1, n_col)
                ]
                by_place = arrays if lane == 1 else arrays[::-1]
                pieces.append([a.reshape(part_blocks, total // 2, side) for a in by_place])
            choices.append(pieces)
        if chunk < chunks:
            result = spread(
                choices, second_values, second_index, result_place, tiles, n_row, total,
                jnp.bfloat16, after,
            )
        else:
            result = collect(
                choices, first_values, first_index, result_place, n_row, total, jnp.bfloat16, after
            )
        panels[chunk] = (result[1], 0, total // 2)
        products[chunk] = result[0]
        return result[0]

    def make_second_grad(after):
        products["second"] = block_grads(
            [panels[c] for c in range(chunks)], grad_views, second_index, second_slots, after
        )
        return products["second"]

    queue = {}
    for chunk in range(1, 2 * chunks):
        queue.setdefault(sum_slots[chunk * parts] - 1, []).append(
            functools.partial(make_terms, chunk)
        )
    for chunk in range(2 * chunks):
        ready = result_slots[(chunk + 1) * parts - 1] + DELAY * last
        queue.setdefault(min(ready, steps), []).append(functools.partial(make_product, chunk))
        if chunk == chunks - 1:
            queue.setdefault(min(ready + 1, steps), []).append(make_second_grad)

    before = [make_terms(0, ())]
    mark = None
    for step in range(steps):
        lanes = []
        for direction in range(2):
            jobs = {k: job(direction, step, k) for k in range(n_col)}
            jobs = {k: found for k, found in jobs.items() if found is not None}
            kind, saved, last_item = None, None, None
            if last in jobs:
                last_item = sum_slots.index(step - DELAY * last)
                kind = "pre" if last_item < items // 2 else "grad"
                saved = kept[direction].get(last_item - items // 2)
            lanes.append(
                {
                    "jobs": jobs,
                    "kind": kind,
                    "saved": saved,
                    "arrived": arrived[direction].get(step - DELAY),
                }
            )
        if any(found != ("on",) for lane in lanes for found in lane["jobs"].values()):
            for direction, (out, pre) in enumerate(
                col_step(position, lanes, last, item_rows, before)
            ):
                made[direction][step] = out
                if pre is not None:
                    kept[direction][last_item] = pre
        else:
            held = in_order([lane["arrived"] for lane in lanes], before)
            for direction in range(2):
                arrived[direction][step - DELAY] = made[direction][step] = held[direction]
        before = []
        mark = made[0][step]
        for direction, pairs in enumerate((up, down)):
            pairs = [pairs[k] for k in lanes[direction]["jobs"] if k < last]
            if pairs:
                arrived[direction][step] = lax.ppermute(made[direction][step], "col", pairs)
        for make in queue.get(step, []):
            before.append(make([mark]))
    for make in queue.get(steps, []):
        before = [make(before[-1:])]

    def scattered(chunk):
        shares = lax.all_to_all(products[chunk], "row", 0, 0)
        return jnp.sum(shares.astype(jnp.float32), axis=0).astype(jnp.bfloat16)

    def joined(first_chunk):
        own_rows = [scattered(first_chunk + c) for c in range(chunks)]
        return jnp.concatenate(own_rows, axis=1).transpose(1, 0, 2).reshape(own, tiles * side)

    outputs = joined(0)
    input_grad = joined(chunks)
    first_grad = block_grads(
        input_views, [panels[chunks + c] for c in range(chunks)], first_index, first_slots, before
    )
    return (outputs, input_grad, first_grad, products["second"])


def solution(mesh):
    placed = (
        P("row", "col"),
        P("col", "row", None, None),
        P("col", "row"),
        P("row", "col", None, None),
        P("row", "col"),
        P("row", "col"),
    )
    return jax.shard_map(
        shards,
        mesh=mesh,
        in_specs=placed,
        out_specs=(
            P("row", "col"),
            P("row", "col"),
            P("col", "row", None, None),
            P("row", "col", None, None),
        ),
        check_vma=False,
    )
```

```python
import functools

import jax
import jax.numpy as jnp
from jax import lax
from jax.experimental import pallas as pl
from jax.experimental.pallas import tpu as pltpu
from jax.sharding import PartitionSpec as P

gelu_scale = 0.7978845608028654
gelu_cubic = 0.044715

CHUNKS = 3
PARTS = 2
DELAY = 2
PIECES = 4
VMEM_BYTES = 64 * 2**20 - 600 * 2**10


def gelu_pair(pre_act):
    inner_arg = gelu_scale * (pre_act + gelu_cubic * pre_act * pre_act * pre_act)
    tanh_value = jnp.tanh(inner_arg)
    activated = 0.5 * pre_act * (1.0 + tanh_value)
    derivative = 0.5 * (1.0 + tanh_value) + 0.5 * pre_act * (
        1.0 - tanh_value * tanh_value
    ) * gelu_scale * (1.0 + 3.0 * gelu_cubic * pre_act * pre_act)
    return (activated, derivative)


def divisor(total, most):
    return max(size for size in range(1, most + 1) if total % size == 0)


def params():
    return pltpu.CompilerParams(
        vmem_limit_bytes=VMEM_BYTES, dimension_semantics=("arbitrary",)
    )


def groups_of(count, width):
    return [list(range(at, min(at + width, count))) for at in range(0, count, width)]


ANY = pl.BlockSpec(memory_space=pl.ANY)


def view_spec(view, blocks, index):
    array, offset, tokens = view
    assert offset % tokens == 0
    shape = (array.shape[0], blocks, tokens, array.shape[3])
    return pl.BlockSpec(shape, lambda i, *refs: (0, index(i), offset // tokens, 0))


def chosen_copies(choices, refs, target, sems):
    copies = []
    at = 0
    for half, lane in enumerate(choices):
        for part, arrays in enumerate(lane):
            blocks = arrays[0].shape[0]
            for place in range(len(arrays)):
                copies.append(
                    (
                        half,
                        place,
                        pltpu.make_async_copy(
                            refs[at],
                            target.at[half, pl.ds(part * blocks, blocks)],
                            sems.at[half, part],
                        ),
                    )
                )
                at += 1
    return copies


def fetch(copies, position_ref):
    for act in ("start", "wait"):
        for half, place, copy in copies:

            @pl.when(position_ref[half] == place)
            def _(copy=copy, act=act):
                getattr(copy, act)()


def product_kernel(
    name, panel, values, index, position, out_shape, out_spec, work, after, resident, sums=None
):
    rows, slots, side = values.shape[:3]
    per = divisor(rows, max(1, 48 // slots))
    chosen = isinstance(panel, list)
    flat = [array for lane in panel for arrays in lane for array in arrays] if chosen else []
    if chosen:
        half_tokens = flat[0].shape[1]
        all_blocks = sum(arrays[0].shape[0] for arrays in panel[0])
        panel_shape = (len(panel), all_blocks, half_tokens, side)
        panel_specs, panel_operands = [ANY] * len(flat), flat
        out_specs = [out_spec(per), ANY]
        out_shapes = [out_shape, jax.ShapeDtypeStruct(panel_shape, jnp.bfloat16)]
        scratch = [
            pltpu.VMEM(panel_shape, jnp.bfloat16),
            pltpu.SemaphoreType.DMA((len(panel), len(panel[0]))),
            pltpu.SemaphoreType.DMA(()),
        ]
    else:
        blocks = panel[0].shape[1]
        spec = view_spec(panel, blocks, lambda i: 0) if resident else view_spec(panel, per, lambda i: i)
        panel_specs, panel_operands = [spec], [panel[0]]
        out_specs, out_shapes, scratch = [out_spec(per)], [out_shape], []
    if sums is not None:
        scratch.append(pltpu.VMEM(sums, jnp.float32))
    total = 2 * flat[0].shape[1] if chosen else panel[0].shape[0] * panel[2]
    last_step = rows // per - 1

    def body(index_ref, position_ref, value_ref, *refs):
        step = pl.program_id(0)
        total_ref = None
        if sums is not None:
            refs, total_ref = refs[:-1], refs[-1]
        if chosen:
            panel_refs = refs[: len(flat)]
            out_ref, kept_ref, held, sems, kept_sem = refs[len(flat) + len(after) :]
            keep = pltpu.make_async_copy(held, kept_ref, kept_sem)

            @pl.when(step == 0)
            def _():
                fetch(chosen_copies(panel, panel_refs, held, sems), position_ref)
                keep.start()

            def read(block, local):
                at = step * per + local if block is None else block
                return held[:, at].reshape(total, side)

        else:
            panel_ref, out_ref = refs[0], refs[1 + len(after)]

            def read(block, local):
                at = local if block is None else block
                return panel_ref[:, at].reshape(total, side)

        work(step, per, read, value_ref, index_ref, out_ref, total_ref)
        if chosen:

            @pl.when(step == last_step)
            def _():
                keep.wait()

    made = pl.pallas_call(
        body,
        grid_spec=pltpu.PrefetchScalarGridSpec(
            num_scalar_prefetch=2,
            grid=(rows // per,),
            in_specs=[pl.BlockSpec((per, slots, side, side), lambda i, *refs: (i, 0, 0, 0))]
            + panel_specs
            + [ANY] * len(after),
            out_specs=out_specs,
            scratch_shapes=scratch,
        ),
        out_shape=out_shapes,
        compiler_params=params(),
        cost_estimate=pl.CostEstimate(flops=2**20, bytes_accessed=2**20, transcendentals=0),
        name=name,
    )(index, position, values, *panel_operands, *after)
    return made if chosen else made[0]


def spread(panel, values, index, position, out_blocks, out_groups, total, dtype, after=()):
    rows, slots, side = values.shape[:3]
    narrow = dtype != jnp.float32
    shape = (out_groups, out_blocks, total // out_groups, side)

    def work(step, per, read, value_ref, index_ref, out_ref, total_ref):
        total_ref = total_ref if narrow else out_ref

        @pl.when(step == 0)
        def _():
            total_ref[...] = jnp.zeros_like(total_ref)

        for local in range(per):
            source = read(None, local)
            for group in groups_of(slots, 2):
                weights = jnp.concatenate([value_ref[local, s] for s in group], axis=1)
                product = jnp.dot(source, weights, preferred_element_type=jnp.float32)
                for at, s in enumerate(group):
                    block = index_ref[(step * per + local) * slots + s]
                    piece = product[:, at * side : (at + 1) * side]
                    total_ref[:, block] += piece.reshape(out_groups, total // out_groups, side)

        if narrow:

            @pl.when(step == rows // per - 1)
            def _():
                for block in range(out_blocks):
                    out_ref[:, block] = total_ref[:, block].astype(dtype)

    return product_kernel(
        "spread",
        panel,
        values,
        index,
        position,
        jax.ShapeDtypeStruct(shape, dtype),
        lambda per: pl.BlockSpec(shape, lambda i, *refs: (0, 0, 0, 0)),
        work,
        list(after),
        False,
        shape if narrow else None,
    )


def collect(panel, values, index, position, out_groups, total, dtype, after=()):
    rows, slots, side = values.shape[:3]
    tokens = total // out_groups

    def work(step, per, read, value_ref, index_ref, out_ref, total_ref):
        for local in range(per):
            picked = [
                read(index_ref[(step * per + local) * slots + s], local) for s in range(slots)
            ]
            weights = jnp.concatenate([value_ref[local, s] for s in range(slots)], axis=1)
            summed = lax.dot_general(
                jnp.concatenate(picked, axis=1),
                weights,
                (((1,), (1,)), ((), ())),
                preferred_element_type=jnp.float32,
            )
            out_ref[:, local] = summed.reshape(out_groups, tokens, side).astype(dtype)

    return product_kernel(
        "collect",
        panel,
        values,
        index,
        position,
        jax.ShapeDtypeStruct((out_groups, rows, tokens, side), dtype),
        lambda per: pl.BlockSpec((out_groups, per, tokens, side), lambda i, *refs: (0, i, 0, 0)),
        work,
        list(after),
        True,
    )


def block_grads(lefts, rights, index, slots, after=(), flops=2**20):
    side = lefts[0][0].shape[3]
    rows = lefts[0][0].shape[1]
    per = divisor(rows, max(1, 24 // slots))
    count = len(lefts)

    def flat(piece):
        return piece.reshape(piece.shape[0] * piece.shape[1], side)

    def body(index_ref, *refs):
        left_refs, right_refs, out_ref = refs[:count], refs[count : 2 * count], refs[-1]
        step = pl.program_id(0)
        for local in range(per):
            left = jnp.concatenate([flat(ref[:, local]) for ref in left_refs], axis=0)
            turned = left.T
            for group in groups_of(slots, 2):
                columns = []
                for s in group:
                    block = index_ref[(step * per + local) * slots + s]
                    columns.append(
                        jnp.concatenate([flat(ref[:, block]) for ref in right_refs], axis=0)
                    )
                product = jnp.dot(
                    turned,
                    jnp.concatenate(columns, axis=1),
                    preferred_element_type=jnp.float32,
                )
                for at, s in enumerate(group):
                    out_ref[local, s] = product[:, at * side : (at + 1) * side].astype(
                        out_ref.dtype
                    )

    left_specs = [view_spec(view, per, lambda i: i) for view in lefts]
    right_specs = [view_spec(view, view[0].shape[1], lambda i: 0) for view in rights]
    return pl.pallas_call(
        body,
        grid_spec=pltpu.PrefetchScalarGridSpec(
            num_scalar_prefetch=1,
            grid=(rows // per,),
            in_specs=left_specs + right_specs + [ANY] * len(after),
            out_specs=pl.BlockSpec((per, slots, side, side), lambda i, *refs: (i, 0, 0, 0)),
        ),
        out_shape=jax.ShapeDtypeStruct((rows, slots, side, side), jnp.bfloat16),
        compiler_params=params(),
        cost_estimate=pl.CostEstimate(flops=flops, bytes_accessed=2**20, transcendentals=0),
        name="block_grads",
    )(index, *[v[0] for v in lefts], *[v[0] for v in rights], *after)


def add_shares(shares, after):
    devices, blocks, _, side = shares[0].shape
    per = divisor(blocks, 4)
    own = sum(array.shape[2] for array in shares)

    def body(*refs):
        out_ref = refs[-1]
        at = 0
        for ref in refs[: len(shares)]:
            tokens = ref.shape[2]
            for block in range(per):
                total = ref[0, block].astype(jnp.float32)
                for device in range(1, devices):
                    total = total + ref[device, block].astype(jnp.float32)
                out_ref[at : at + tokens, block * side : (block + 1) * side] = total.astype(
                    out_ref.dtype
                )
            at += tokens

    return pl.pallas_call(
        body,
        grid=(blocks // per,),
        in_specs=[
            pl.BlockSpec((devices, per, a.shape[2], side), lambda i: (0, i, 0, 0)) for a in shares
        ]
        + [ANY] * len(after),
        out_specs=pl.BlockSpec((own, per * side), lambda i: (0, i)),
        out_shape=jax.ShapeDtypeStruct((own, blocks * side), jnp.bfloat16),
        compiler_params=params(),
        cost_estimate=pl.CostEstimate(flops=2**20, bytes_accessed=2**20, transcendentals=0),
        name="add_shares",
    )(*shares, *after)


def col_step(position, lanes, last, rows, after):
    side = 128
    size = rows // PIECES
    operands, out_shapes, plan = [], [], []

    def operand(array):
        if array is None:
            return None
        operands.append(array)
        return len(operands) - 1

    def result(dtype):
        out_shapes.append(jax.ShapeDtypeStruct((rows, side), dtype))
        return len(out_shapes) - 1

    for lane in lanes:
        jobs = {}
        for place, job in lane["jobs"].items():
            jobs[place] = (job[0],) if len(job) == 1 else (job[0], operand(job[1])) + job[2:]
        plan.append(
            {
                "jobs": jobs,
                "kind": lane["kind"],
                "arrived": operand(lane["arrived"]),
                "saved": operand(lane["saved"]) if lane["kind"] == "grad" else None,
                "out": result(jnp.bfloat16),
                "kept": result(jnp.float32) if lane["kind"] == "pre" else None,
            }
        )
    n_in = len(operands)
    n_out = len(out_shapes)

    def body(position_ref, *refs):
        ins, outs = refs[:n_in], refs[n_in + len(after) : n_in + len(after) + n_out]
        arrived, terms, third, ready, load_sem, store_sem = refs[n_in + len(after) + n_out :]

        def loads(which, lane, place, piece):
            span = pl.ds(piece * size, size)
            job = lane["jobs"][place]

            def load(source, target, kind):
                return pltpu.make_async_copy(
                    source, target.at[which, span], load_sem.at[which, kind, piece]
                )

            if job[0] == "fresh":
                return [load(ins[job[1]].at[span], ready, 0)]
            if job[0] == "on":
                return [load(ins[lane["arrived"]].at[span], ready, 0)]
            array, half, part = job[1:]
            own = pl.ds(part * rows + piece * size, size)
            copies = [load(ins[array].at[half, own], terms, 0)]
            if place > 0:
                copies.append(load(ins[lane["arrived"]].at[span], arrived, 1))
            if place == last and lane["kind"] == "grad":
                copies.append(load(ins[lane["saved"]].at[span], third, 2))
            return copies

        def stores(which, lane, place, piece):
            span = pl.ds(piece * size, size)
            copies = [
                pltpu.make_async_copy(
                    ready.at[which, span], outs[lane["out"]].at[span], store_sem.at[which, 0, piece]
                )
            ]
            if place == last and lane["kind"] == "pre":
                copies.append(
                    pltpu.make_async_copy(
                        third.at[which, span],
                        outs[lane["kept"]].at[span],
                        store_sem.at[which, 1, piece],
                    )
                )
            return copies

        def each(act):
            for which, lane in enumerate(plan):
                for place in lane["jobs"]:

                    @pl.when(position_ref[which] == place)
                    def _(which=which, lane=lane, place=place):
                        act(which, lane, place)

        def start_all(which, lane, place):
            for piece in range(PIECES):
                for copy in loads(which, lane, place, piece):
                    copy.start()

        def work_all(which, lane, place):
            for piece in range(PIECES):
                for copy in loads(which, lane, place, piece):
                    copy.wait()
                span = pl.ds(piece * size, size)
                if lane["jobs"][place][0] == "sum":
                    total = terms[which, span]
                    if place > 0:
                        total = total + arrived[which, span].astype(jnp.float32)
                    if place == last and lane["kind"] == "pre":
                        third[which, span] = total
                        total = gelu_pair(total)[0]
                    elif place == last:
                        total = total * gelu_pair(third[which, span])[1]
                    ready[which, span] = total.astype(jnp.bfloat16)
                for copy in stores(which, lane, place, piece):
                    copy.start()

        def wait_all(which, lane, place):
            for piece in range(PIECES):
                for copy in stores(which, lane, place, piece):
                    copy.wait()

        each(start_all)
        each(work_all)
        each(wait_all)

    made = pl.pallas_call(
        body,
        grid_spec=pltpu.PrefetchScalarGridSpec(
            num_scalar_prefetch=1,
            grid=(1,),
            in_specs=[ANY] * (n_in + len(after)),
            out_specs=[ANY] * n_out,
            scratch_shapes=[
                pltpu.VMEM((2, rows, side), jnp.bfloat16),
                pltpu.VMEM((2, rows, side), jnp.float32),
                pltpu.VMEM((2, rows, side), jnp.float32),
                pltpu.VMEM((2, rows, side), jnp.bfloat16),
                pltpu.SemaphoreType.DMA((2, 3, PIECES)),
                pltpu.SemaphoreType.DMA((2, 2, PIECES)),
            ],
        ),
        out_shape=out_shapes,
        compiler_params=params(),
        cost_estimate=pl.CostEstimate(flops=2**20, bytes_accessed=2**20, transcendentals=0),
        name="col_step",
    )(position, *operands, *after)
    return [
        (made[lane["out"]], None if lane["kept"] is None else made[lane["kept"]]) for lane in plan
    ]


def in_order(arrays, after):
    def body(*refs):
        pass

    return pl.pallas_call(
        body,
        in_specs=[ANY] * (len(arrays) + len(after)),
        out_specs=[ANY] * len(arrays),
        out_shape=[jax.ShapeDtypeStruct(a.shape, a.dtype) for a in arrays],
        input_output_aliases={k: k for k in range(len(arrays))},
        cost_estimate=pl.CostEstimate(flops=1024, bytes_accessed=1024, transcendentals=0),
        compiler_params=pltpu.CompilerParams(vmem_limit_bytes=VMEM_BYTES),
        name="in_order",
    )(*arrays, *after)


def link_order(items, last):
    sums, results, slot, sum_turn = [], [], 0, True
    while len(results) < items:
        more_sums = len(sums) < items
        can_pass = len(results) < len(sums) and slot > sums[len(results)] + DELAY * last
        if more_sums and (len(sums) < items // 2 or sum_turn or not can_pass):
            sums.append(slot)
            sum_turn = False
        elif can_pass:
            results.append(slot)
            sum_turn = True
        slot += 1
    return sums, results


def shards(inputs, first_values, first_blocks, second_values, second_blocks, cotangent):
    n_row, n_col = lax.axis_size("row"), lax.axis_size("col")
    last = n_col - 1
    tiles, first_slots, side = first_values.shape[:3]
    hidden, second_slots = second_values.shape[:2]
    own = inputs.shape[0]
    chunks = divisor(own // 16, CHUNKS)
    parts = divisor(hidden, PARTS)
    part_blocks = hidden // parts
    rows = own // chunks
    total = rows * n_row
    item_rows = part_blocks * total // 2

    first_index = (first_blocks - lax.axis_index("row") * hidden).reshape(-1)
    second_index = (second_blocks - lax.axis_index("col") * tiles).reshape(-1)
    place = lax.axis_index("col").astype(jnp.int32)
    position = jnp.stack([place, last - place])
    result_place = jnp.stack([place, place])

    def by_block(array):
        return array.reshape(own, tiles, side).transpose(1, 0, 2)

    first = by_block(inputs)
    opening = lax.all_gather(first[:, :rows], "row")
    input_views = [(opening, 0, rows)]
    if chunks > 1:
        others = lax.all_gather(first[:, rows:], "row")
        input_views += [(others, at * rows, rows) for at in range(chunks - 1)]
    gathered = lax.all_gather(by_block(cotangent), "row")
    grad_views = [(gathered, at * rows, rows) for at in range(chunks)]

    items = 2 * chunks * parts
    sum_slots, result_slots = link_order(items, last)
    steps = result_slots[-1] + DELAY * (last - 1) + 1

    terms = {}
    panels = {}
    products = {}
    made = [{}, {}]
    kept = [{}, {}]
    arrived = [{}, {}]
    halves = (1, 0)
    up = [(k, k + 1) for k in range(last)]
    down = [(last - k, last - k - 1) for k in range(last)]

    def job(direction, step, k):
        slot = step - DELAY * k
        if slot in sum_slots:
            item = sum_slots.index(slot)
            return ("sum", terms[item // parts], halves[direction], item % parts)
        if slot in result_slots and k < last:
            item = result_slots.index(slot)
            if k > 0:
                return ("on",)
            return ("fresh", made[1 - direction][sum_slots[item] + DELAY * last])
        return None

    def make_terms(chunk, after):
        if chunk < chunks:
            result = spread(
                input_views[chunk], first_values, first_index, position, hidden, 2, total,
                jnp.float32, after,
            )
        else:
            result = collect(
                grad_views[chunk - chunks], second_values, second_index, position, 2, total,
                jnp.float32, after,
            )
        terms[chunk] = result.reshape(2, hidden * total // 2, side)
        return result

    def make_product(chunk, after):
        choices = []
        for half in range(2):
            lane = halves.index(half)
            pieces = []
            for part in range(parts):
                item = chunk * parts + part
                arrays = [made[lane][sum_slots[item] + DELAY * last]] + [
                    arrived[1 - lane][result_slots[item] + DELAY * (hop - 1)]
                    for hop in range(1, n_col)
                ]
                by_place = arrays if lane == 1 else arrays[::-1]
                pieces.append([a.reshape(part_blocks, total // 2, side) for a in by_place])
            choices.append(pieces)
        if chunk < chunks:
            result = spread(
                choices, second_values, second_index, result_place, tiles, n_row, total,
                jnp.bfloat16, after,
            )
        else:
            result = collect(
                choices, first_values, first_index, result_place, n_row, total, jnp.bfloat16, after
            )
        panels[chunk] = (result[1], 0, total // 2)
        products[chunk] = result[0]
        return result[0]

    def make_second_grad(after):
        products["second"] = block_grads(
            [panels[c] for c in range(chunks)], grad_views, second_index, second_slots, after
        )
        return products["second"]

    queue = {}
    for chunk in range(1, 2 * chunks):
        queue.setdefault(sum_slots[chunk * parts] - 1, []).append(
            functools.partial(make_terms, chunk)
        )
    for chunk in range(2 * chunks):
        ready = result_slots[(chunk + 1) * parts - 1] + DELAY * last
        ready += ready >= result_slots[-1]
        ready = min(ready, steps + DELAY - 1)
        queue.setdefault(ready, []).append(functools.partial(make_product, chunk))
        if chunk == chunks - 1:
            queue.setdefault(max(ready, steps - 1), []).append(make_second_grad)

    before = [make_terms(0, ())]
    mark = None
    for step in range(steps):
        lanes = []
        for direction in range(2):
            jobs = {k: job(direction, step, k) for k in range(n_col)}
            jobs = {k: found for k, found in jobs.items() if found is not None}
            kind, saved, last_item = None, None, None
            if last in jobs:
                last_item = sum_slots.index(step - DELAY * last)
                kind = "pre" if last_item < items // 2 else "grad"
                saved = kept[direction].get(last_item - items // 2)
            lanes.append(
                {
                    "jobs": jobs,
                    "kind": kind,
                    "saved": saved,
                    "arrived": arrived[direction].get(step - DELAY),
                }
            )
        if any(found != ("on",) for lane in lanes for found in lane["jobs"].values()):
            for direction, (out, pre) in enumerate(
                col_step(position, lanes, last, item_rows, before)
            ):
                made[direction][step] = out
                if pre is not None:
                    kept[direction][last_item] = pre
        else:
            held = in_order([lane["arrived"] for lane in lanes], before)
            for direction in range(2):
                arrived[direction][step - DELAY] = made[direction][step] = held[direction]
        before = []
        mark = made[0][step]
        for direction, pairs in enumerate((up, down)):
            pairs = [pairs[k] for k in lanes[direction]["jobs"] if k < last]
            if pairs:
                arrived[direction][step] = lax.ppermute(made[direction][step], "col", pairs)
        for make in queue.get(step, []):
            before.append(make([mark]))
    for step in range(steps, steps + DELAY):
        held = in_order([arrived[direction][step - DELAY] for direction in range(2)], before)
        for direction in range(2):
            arrived[direction][step - DELAY] = held[direction]
        before, mark = [], held[0]
        for make in queue.get(step, []):
            before.append(make([mark] + before[-1:]))

    shares = [lax.all_to_all(products[c], "row", 0, 0) for c in range(2 * chunks)]
    first_grad = block_grads(
        input_views,
        [panels[chunks + c] for c in range(chunks)],
        first_index,
        first_slots,
        before,
        2**38,
    )
    outputs = add_shares(shares[:chunks], [first_grad])
    input_grad = add_shares(shares[chunks:], [first_grad])
    return (outputs, input_grad, first_grad, products["second"])


def solution(mesh):
    placed = (
        P("row", "col"),
        P("col", "row", None, None),
        P("col", "row"),
        P("row", "col", None, None),
        P("row", "col"),
        P("row", "col"),
    )
    return jax.shard_map(
        shards,
        mesh=mesh,
        in_specs=placed,
        out_specs=(
            P("row", "col"),
            P("row", "col"),
            P("col", "row", None, None),
            P("row", "col", None, None),
        ),
        check_vma=False,
    )
```

```python
import functools

import jax
import jax.numpy as jnp
from jax import lax
from jax.experimental import pallas as pl
from jax.experimental.pallas import tpu as pltpu
from jax.sharding import PartitionSpec as P

gelu_scale = 0.7978845608028654
gelu_cubic = 0.044715

CHUNKS = 3
PARTS = 2
DELAY = 2
PIECES = 4
VMEM_BYTES = 64 * 2**20 - 600 * 2**10


def gelu_pair(pre_act):
    inner_arg = gelu_scale * (pre_act + gelu_cubic * pre_act * pre_act * pre_act)
    tanh_value = jnp.tanh(inner_arg)
    activated = 0.5 * pre_act * (1.0 + tanh_value)
    derivative = 0.5 * (1.0 + tanh_value) + 0.5 * pre_act * (
        1.0 - tanh_value * tanh_value
    ) * gelu_scale * (1.0 + 3.0 * gelu_cubic * pre_act * pre_act)
    return (activated, derivative)


def divisor(total, most):
    return max(size for size in range(1, most + 1) if total % size == 0)


def params():
    return pltpu.CompilerParams(
        vmem_limit_bytes=VMEM_BYTES, dimension_semantics=("arbitrary",)
    )


def groups_of(count, width):
    return [list(range(at, min(at + width, count))) for at in range(0, count, width)]


ANY = pl.BlockSpec(memory_space=pl.ANY)


def view_spec(view, blocks, index):
    array, offset, tokens = view
    assert offset % tokens == 0
    shape = (array.shape[0], blocks, tokens, array.shape[3])
    return pl.BlockSpec(shape, lambda i, *refs: (0, index(i), offset // tokens, 0))


def chosen_copies(choices, refs, target, sems):
    copies = []
    at = 0
    for half, lane in enumerate(choices):
        for part, arrays in enumerate(lane):
            blocks = arrays[0].shape[0]
            for place in range(len(arrays)):
                copies.append(
                    (
                        half,
                        place,
                        pltpu.make_async_copy(
                            refs[at],
                            target.at[half, pl.ds(part * blocks, blocks)],
                            sems.at[half, part],
                        ),
                    )
                )
                at += 1
    return copies


def fetch(copies, position_ref):
    for act in ("start", "wait"):
        for half, place, copy in copies:

            @pl.when(position_ref[half] == place)
            def _(copy=copy, act=act):
                getattr(copy, act)()


def product_kernel(
    name, panel, values, index, position, out_shape, out_spec, work, after, resident, sums=None
):
    flops = 2**35 if isinstance(panel, list) else 2**20
    rows, slots, side = values.shape[:3]
    per = divisor(rows, max(1, 48 // slots))
    chosen = isinstance(panel, list)
    flat = [array for lane in panel for arrays in lane for array in arrays] if chosen else []
    if chosen:
        half_tokens = flat[0].shape[1]
        all_blocks = sum(arrays[0].shape[0] for arrays in panel[0])
        panel_shape = (len(panel), all_blocks, half_tokens, side)
        panel_specs, panel_operands = [ANY] * len(flat), flat
        out_specs = [out_spec(per), ANY]
        out_shapes = [out_shape, jax.ShapeDtypeStruct(panel_shape, jnp.bfloat16)]
        scratch = [
            pltpu.VMEM(panel_shape, jnp.bfloat16),
            pltpu.SemaphoreType.DMA((len(panel), len(panel[0]))),
            pltpu.SemaphoreType.DMA(()),
        ]
    else:
        blocks = panel[0].shape[1]
        spec = view_spec(panel, blocks, lambda i: 0) if resident else view_spec(panel, per, lambda i: i)
        panel_specs, panel_operands = [spec], [panel[0]]
        out_specs, out_shapes, scratch = [out_spec(per)], [out_shape], []
    if sums is not None:
        scratch.append(pltpu.VMEM(sums, jnp.float32))
    total = 2 * flat[0].shape[1] if chosen else panel[0].shape[0] * panel[2]
    last_step = rows // per - 1

    def body(index_ref, position_ref, value_ref, *refs):
        step = pl.program_id(0)
        total_ref = None
        if sums is not None:
            refs, total_ref = refs[:-1], refs[-1]
        if chosen:
            panel_refs = refs[: len(flat)]
            out_ref, kept_ref, held, sems, kept_sem = refs[len(flat) + len(after) :]
            keep = pltpu.make_async_copy(held, kept_ref, kept_sem)

            @pl.when(step == 0)
            def _():
                fetch(chosen_copies(panel, panel_refs, held, sems), position_ref)
                keep.start()

            def read(block, local):
                at = step * per + local if block is None else block
                return held[:, at].reshape(total, side)

        else:
            panel_ref, out_ref = refs[0], refs[1 + len(after)]

            def read(block, local):
                at = local if block is None else block
                return panel_ref[:, at].reshape(total, side)

        work(step, per, read, value_ref, index_ref, out_ref, total_ref)
        if chosen:

            @pl.when(step == last_step)
            def _():
                keep.wait()

    made = pl.pallas_call(
        body,
        grid_spec=pltpu.PrefetchScalarGridSpec(
            num_scalar_prefetch=2,
            grid=(rows // per,),
            in_specs=[pl.BlockSpec((per, slots, side, side), lambda i, *refs: (i, 0, 0, 0))]
            + panel_specs
            + [ANY] * len(after),
            out_specs=out_specs,
            scratch_shapes=scratch,
        ),
        out_shape=out_shapes,
        compiler_params=params(),
        cost_estimate=pl.CostEstimate(flops=flops, bytes_accessed=2**20, transcendentals=0),
        name=name,
    )(index, position, values, *panel_operands, *after)
    return made if chosen else made[0]


def spread(panel, values, index, position, out_blocks, out_groups, total, dtype, after=()):
    rows, slots, side = values.shape[:3]
    narrow = dtype != jnp.float32
    shape = (out_groups, out_blocks, total // out_groups, side)

    def work(step, per, read, value_ref, index_ref, out_ref, total_ref):
        total_ref = total_ref if narrow else out_ref

        @pl.when(step == 0)
        def _():
            total_ref[...] = jnp.zeros_like(total_ref)

        for local in range(per):
            source = read(None, local)
            for group in groups_of(slots, 2):
                weights = jnp.concatenate([value_ref[local, s] for s in group], axis=1)
                product = jnp.dot(source, weights, preferred_element_type=jnp.float32)
                for at, s in enumerate(group):
                    block = index_ref[(step * per + local) * slots + s]
                    piece = product[:, at * side : (at + 1) * side]
                    total_ref[:, block] += piece.reshape(out_groups, total // out_groups, side)

        if narrow:

            @pl.when(step == rows // per - 1)
            def _():
                for block in range(out_blocks):
                    out_ref[:, block] = total_ref[:, block].astype(dtype)

    return product_kernel(
        "spread",
        panel,
        values,
        index,
        position,
        jax.ShapeDtypeStruct(shape, dtype),
        lambda per: pl.BlockSpec(shape, lambda i, *refs: (0, 0, 0, 0)),
        work,
        list(after),
        False,
        shape if narrow else None,
    )


def collect(panel, values, index, position, out_groups, total, dtype, after=()):
    rows, slots, side = values.shape[:3]
    tokens = total // out_groups

    def work(step, per, read, value_ref, index_ref, out_ref, total_ref):
        for local in range(per):
            picked = [
                read(index_ref[(step * per + local) * slots + s], local) for s in range(slots)
            ]
            weights = jnp.concatenate([value_ref[local, s] for s in range(slots)], axis=1)
            summed = lax.dot_general(
                jnp.concatenate(picked, axis=1),
                weights,
                (((1,), (1,)), ((), ())),
                preferred_element_type=jnp.float32,
            )
            out_ref[:, local] = summed.reshape(out_groups, tokens, side).astype(dtype)

    return product_kernel(
        "collect",
        panel,
        values,
        index,
        position,
        jax.ShapeDtypeStruct((out_groups, rows, tokens, side), dtype),
        lambda per: pl.BlockSpec((out_groups, per, tokens, side), lambda i, *refs: (0, i, 0, 0)),
        work,
        list(after),
        True,
    )


def block_grads(lefts, rights, index, slots, after=(), flops=2**20):
    side = lefts[0][0].shape[3]
    rows = lefts[0][0].shape[1]
    per = divisor(rows, max(1, 24 // slots))
    count = len(lefts)

    def flat(piece):
        return piece.reshape(piece.shape[0] * piece.shape[1], side)

    def body(index_ref, *refs):
        left_refs, right_refs, out_ref = refs[:count], refs[count : 2 * count], refs[-1]
        step = pl.program_id(0)
        for local in range(per):
            left = jnp.concatenate([flat(ref[:, local]) for ref in left_refs], axis=0)
            turned = left.T
            for group in groups_of(slots, 2):
                columns = []
                for s in group:
                    block = index_ref[(step * per + local) * slots + s]
                    columns.append(
                        jnp.concatenate([flat(ref[:, block]) for ref in right_refs], axis=0)
                    )
                product = jnp.dot(
                    turned,
                    jnp.concatenate(columns, axis=1),
                    preferred_element_type=jnp.float32,
                )
                for at, s in enumerate(group):
                    out_ref[local, s] = product[:, at * side : (at + 1) * side].astype(
                        out_ref.dtype
                    )

    left_specs = [view_spec(view, per, lambda i: i) for view in lefts]
    right_specs = [view_spec(view, view[0].shape[1], lambda i: 0) for view in rights]
    return pl.pallas_call(
        body,
        grid_spec=pltpu.PrefetchScalarGridSpec(
            num_scalar_prefetch=1,
            grid=(rows // per,),
            in_specs=left_specs + right_specs + [ANY] * len(after),
            out_specs=pl.BlockSpec((per, slots, side, side), lambda i, *refs: (i, 0, 0, 0)),
        ),
        out_shape=jax.ShapeDtypeStruct((rows, slots, side, side), jnp.bfloat16),
        compiler_params=params(),
        cost_estimate=pl.CostEstimate(flops=flops, bytes_accessed=2**20, transcendentals=0),
        name="block_grads",
    )(index, *[v[0] for v in lefts], *[v[0] for v in rights], *after)


def add_shares(shares, after):
    devices, blocks, _, side = shares[0].shape
    per = divisor(blocks, 4)
    own = sum(array.shape[2] for array in shares)

    def body(*refs):
        out_ref = refs[-1]
        at = 0
        for ref in refs[: len(shares)]:
            tokens = ref.shape[2]
            for block in range(per):
                total = ref[0, block].astype(jnp.float32)
                for device in range(1, devices):
                    total = total + ref[device, block].astype(jnp.float32)
                out_ref[at : at + tokens, block * side : (block + 1) * side] = total.astype(
                    out_ref.dtype
                )
            at += tokens

    return pl.pallas_call(
        body,
        grid=(blocks // per,),
        in_specs=[
            pl.BlockSpec((devices, per, a.shape[2], side), lambda i: (0, i, 0, 0)) for a in shares
        ]
        + [ANY] * len(after),
        out_specs=pl.BlockSpec((own, per * side), lambda i: (0, i)),
        out_shape=jax.ShapeDtypeStruct((own, blocks * side), jnp.bfloat16),
        compiler_params=params(),
        cost_estimate=pl.CostEstimate(flops=2**20, bytes_accessed=2**20, transcendentals=0),
        name="add_shares",
    )(*shares, *after)


def col_step(position, lanes, last, rows, after):
    side = 128
    size = rows // PIECES
    operands, out_shapes, plan = [], [], []

    def operand(array):
        if array is None:
            return None
        operands.append(array)
        return len(operands) - 1

    def result(dtype):
        out_shapes.append(jax.ShapeDtypeStruct((rows, side), dtype))
        return len(out_shapes) - 1

    for lane in lanes:
        jobs = {}
        for place, job in lane["jobs"].items():
            jobs[place] = (job[0],) if len(job) == 1 else (job[0], operand(job[1])) + job[2:]
        plan.append(
            {
                "jobs": jobs,
                "kind": lane["kind"],
                "arrived": operand(lane["arrived"]),
                "saved": operand(lane["saved"]) if lane["kind"] == "grad" else None,
                "out": result(jnp.bfloat16),
                "kept": result(jnp.float32) if lane["kind"] == "pre" else None,
            }
        )
    n_in = len(operands)
    n_out = len(out_shapes)

    def body(position_ref, *refs):
        ins, outs = refs[:n_in], refs[n_in + len(after) : n_in + len(after) + n_out]
        arrived, terms, third, ready, load_sem, store_sem = refs[n_in + len(after) + n_out :]

        def loads(which, lane, place, piece):
            span = pl.ds(piece * size, size)
            job = lane["jobs"][place]

            def load(source, target, kind):
                return pltpu.make_async_copy(
                    source, target.at[which, span], load_sem.at[which, kind, piece]
                )

            if job[0] == "fresh":
                return [load(ins[job[1]].at[span], ready, 0)]
            if job[0] == "on":
                return [load(ins[lane["arrived"]].at[span], ready, 0)]
            array, half, part = job[1:]
            own = pl.ds(part * rows + piece * size, size)
            copies = [load(ins[array].at[half, own], terms, 0)]
            if place > 0:
                copies.append(load(ins[lane["arrived"]].at[span], arrived, 1))
            if place == last and lane["kind"] == "grad":
                copies.append(load(ins[lane["saved"]].at[span], third, 2))
            return copies

        def stores(which, lane, place, piece):
            span = pl.ds(piece * size, size)
            copies = [
                pltpu.make_async_copy(
                    ready.at[which, span], outs[lane["out"]].at[span], store_sem.at[which, 0, piece]
                )
            ]
            if place == last and lane["kind"] == "pre":
                copies.append(
                    pltpu.make_async_copy(
                        third.at[which, span],
                        outs[lane["kept"]].at[span],
                        store_sem.at[which, 1, piece],
                    )
                )
            return copies

        def each(act):
            for which, lane in enumerate(plan):
                for place in lane["jobs"]:

                    @pl.when(position_ref[which] == place)
                    def _(which=which, lane=lane, place=place):
                        act(which, lane, place)

        def start_all(which, lane, place):
            for piece in range(PIECES):
                for copy in loads(which, lane, place, piece):
                    copy.start()

        def work_all(which, lane, place):
            for piece in range(PIECES):
                for copy in loads(which, lane, place, piece):
                    copy.wait()
                span = pl.ds(piece * size, size)
                if lane["jobs"][place][0] == "sum":
                    total = terms[which, span]
                    if place > 0:
                        total = total + arrived[which, span].astype(jnp.float32)
                    if place == last and lane["kind"] == "pre":
                        third[which, span] = total
                        total = gelu_pair(total)[0]
                    elif place == last:
                        total = total * gelu_pair(third[which, span])[1]
                    ready[which, span] = total.astype(jnp.bfloat16)
                for copy in stores(which, lane, place, piece):
                    copy.start()

        def wait_all(which, lane, place):
            for piece in range(PIECES):
                for copy in stores(which, lane, place, piece):
                    copy.wait()

        each(start_all)
        each(work_all)
        each(wait_all)

    made = pl.pallas_call(
        body,
        grid_spec=pltpu.PrefetchScalarGridSpec(
            num_scalar_prefetch=1,
            grid=(1,),
            in_specs=[ANY] * (n_in + len(after)),
            out_specs=[ANY] * n_out,
            scratch_shapes=[
                pltpu.VMEM((2, rows, side), jnp.bfloat16),
                pltpu.VMEM((2, rows, side), jnp.float32),
                pltpu.VMEM((2, rows, side), jnp.float32),
                pltpu.VMEM((2, rows, side), jnp.bfloat16),
                pltpu.SemaphoreType.DMA((2, 3, PIECES)),
                pltpu.SemaphoreType.DMA((2, 2, PIECES)),
            ],
        ),
        out_shape=out_shapes,
        compiler_params=params(),
        cost_estimate=pl.CostEstimate(flops=2**20, bytes_accessed=2**20, transcendentals=0),
        name="col_step",
    )(position, *operands, *after)
    return [
        (made[lane["out"]], None if lane["kept"] is None else made[lane["kept"]]) for lane in plan
    ]


def in_order(arrays, after):
    def body(*refs):
        pass

    return pl.pallas_call(
        body,
        in_specs=[ANY] * (len(arrays) + len(after)),
        out_specs=[ANY] * len(arrays),
        out_shape=[jax.ShapeDtypeStruct(a.shape, a.dtype) for a in arrays],
        input_output_aliases={k: k for k in range(len(arrays))},
        cost_estimate=pl.CostEstimate(flops=1024, bytes_accessed=1024, transcendentals=0),
        compiler_params=pltpu.CompilerParams(vmem_limit_bytes=VMEM_BYTES),
        name="in_order",
    )(*arrays, *after)


def link_order(items, last):
    sums, results, slot, sum_turn = [], [], 0, True
    while len(results) < items:
        more_sums = len(sums) < items
        can_pass = len(results) < len(sums) and slot > sums[len(results)] + DELAY * last
        if more_sums and (len(sums) < items // 2 or sum_turn or not can_pass):
            sums.append(slot)
            sum_turn = False
        elif can_pass:
            results.append(slot)
            sum_turn = True
        slot += 1
    return sums, results


def shards(inputs, first_values, first_blocks, second_values, second_blocks, cotangent):
    n_row, n_col = lax.axis_size("row"), lax.axis_size("col")
    last = n_col - 1
    tiles, first_slots, side = first_values.shape[:3]
    hidden, second_slots = second_values.shape[:2]
    own = inputs.shape[0]
    chunks = divisor(own // 16, CHUNKS)
    parts = divisor(hidden, PARTS)
    part_blocks = hidden // parts
    rows = own // chunks
    total = rows * n_row
    item_rows = part_blocks * total // 2

    first_index = (first_blocks - lax.axis_index("row") * hidden).reshape(-1)
    second_index = (second_blocks - lax.axis_index("col") * tiles).reshape(-1)
    place = lax.axis_index("col").astype(jnp.int32)
    position = jnp.stack([place, last - place])
    result_place = jnp.stack([place, place])

    def by_block(array):
        return array.reshape(own, tiles, side).transpose(1, 0, 2)

    first = by_block(inputs)
    opening = lax.all_gather(first[:, :rows], "row")
    input_views = [(opening, 0, rows)]
    if chunks > 1:
        others = lax.all_gather(first[:, rows:], "row")
        input_views += [(others, at * rows, rows) for at in range(chunks - 1)]
    gathered = lax.all_gather(by_block(cotangent), "row")
    grad_views = [(gathered, at * rows, rows) for at in range(chunks)]

    items = 2 * chunks * parts
    sum_slots, result_slots = link_order(items, last)
    steps = result_slots[-1] + DELAY * (last - 1) + 1

    terms = {}
    panels = {}
    products = {}
    made = [{}, {}]
    kept = [{}, {}]
    arrived = [{}, {}]
    halves = (1, 0)
    up = [(k, k + 1) for k in range(last)]
    down = [(last - k, last - k - 1) for k in range(last)]

    def job(direction, step, k):
        slot = step - DELAY * k
        if slot in sum_slots:
            item = sum_slots.index(slot)
            return ("sum", terms[item // parts], halves[direction], item % parts)
        if slot in result_slots and k < last:
            item = result_slots.index(slot)
            if k > 0:
                return ("on",)
            return ("fresh", made[1 - direction][sum_slots[item] + DELAY * last])
        return None

    def make_terms(chunk, after):
        if chunk < chunks:
            result = spread(
                input_views[chunk], first_values, first_index, position, hidden, 2, total,
                jnp.float32, after,
            )
        else:
            result = collect(
                grad_views[chunk - chunks], second_values, second_index, position, 2, total,
                jnp.float32, after,
            )
        terms[chunk] = result.reshape(2, hidden * total // 2, side)
        return result

    def make_product(chunk, after):
        choices = []
        for half in range(2):
            lane = halves.index(half)
            pieces = []
            for part in range(parts):
                item = chunk * parts + part
                arrays = [made[lane][sum_slots[item] + DELAY * last]] + [
                    arrived[1 - lane][result_slots[item] + DELAY * (hop - 1)]
                    for hop in range(1, n_col)
                ]
                by_place = arrays if lane == 1 else arrays[::-1]
                pieces.append([a.reshape(part_blocks, total // 2, side) for a in by_place])
            choices.append(pieces)
        if chunk < chunks:
            result = spread(
                choices, second_values, second_index, result_place, tiles, n_row, total,
                jnp.bfloat16, after,
            )
        else:
            result = collect(
                choices, first_values, first_index, result_place, n_row, total, jnp.bfloat16, after
            )
        panels[chunk] = (result[1], 0, total // 2)
        products[chunk] = result[0]
        return result[0]

    def make_second_grad(after):
        products["second"] = block_grads(
            [panels[c] for c in range(chunks)], grad_views, second_index, second_slots, after
        )
        return products["second"]

    queue = {}
    for chunk in range(1, 2 * chunks):
        queue.setdefault(sum_slots[chunk * parts] - 1, []).append(
            functools.partial(make_terms, chunk)
        )
    for chunk in range(2 * chunks):
        ready = result_slots[(chunk + 1) * parts - 1] + DELAY * last
        ready += ready >= result_slots[-1]
        ready = min(ready, steps + DELAY - 1)
        queue.setdefault(ready, []).append(functools.partial(make_product, chunk))
        if chunk == chunks - 1:
            queue.setdefault(max(ready, steps - 1), []).append(make_second_grad)

    before = [make_terms(0, ())]
    mark = []
    for step in range(steps):
        lanes = []
        for direction in range(2):
            jobs = {k: job(direction, step, k) for k in range(n_col)}
            jobs = {k: found for k, found in jobs.items() if found is not None}
            kind, saved, last_item = None, None, None
            if last in jobs:
                last_item = sum_slots.index(step - DELAY * last)
                kind = "pre" if last_item < items // 2 else "grad"
                saved = kept[direction].get(last_item - items // 2)
            lanes.append(
                {
                    "jobs": jobs,
                    "kind": kind,
                    "saved": saved,
                    "arrived": arrived[direction].get(step - DELAY),
                }
            )
        if any(found != ("on",) for lane in lanes for found in lane["jobs"].values()):
            for direction, (out, pre) in enumerate(
                col_step(position, lanes, last, item_rows, before + mark)
            ):
                made[direction][step] = out
                if pre is not None:
                    kept[direction][last_item] = pre
        else:
            held = in_order([lane["arrived"] for lane in lanes], before + mark)
            for direction in range(2):
                arrived[direction][step - DELAY] = made[direction][step] = held[direction]
        before = []
        mark = [made[0][step]]
        for direction, pairs in enumerate((up, down)):
            pairs = [pairs[k] for k in lanes[direction]["jobs"] if k < last]
            if pairs:
                arrived[direction][step] = lax.ppermute(made[direction][step], "col", pairs)
        for make in queue.get(step, []):
            before.append(make(mark))
    for step in range(steps, steps + DELAY):
        held = in_order([arrived[direction][step - DELAY] for direction in range(2)], before + mark)
        for direction in range(2):
            arrived[direction][step - DELAY] = held[direction]
        before, mark = [], [held[0]]
        for make in queue.get(step, []):
            before.append(make(mark + before[-1:]))

    shares = []
    for chunk in range(2 * chunks):
        product = products[chunk]
        if shares:
            (product,) = in_order([product], shares[-1:])
        shares.append(lax.all_to_all(product, "row", 0, 0))
    first_grad = block_grads(
        input_views,
        [panels[chunks + c] for c in range(chunks)],
        first_index,
        first_slots,
        [product],
        2**38,
    )
    outputs = add_shares(shares[:chunks], [first_grad])
    input_grad = add_shares(shares[chunks:], [first_grad])
    return (outputs, input_grad, first_grad, products["second"])


def solution(mesh):
    placed = (
        P("row", "col"),
        P("col", "row", None, None),
        P("col", "row"),
        P("row", "col", None, None),
        P("row", "col"),
        P("row", "col"),
    )
    return jax.shard_map(
        shards,
        mesh=mesh,
        in_specs=placed,
        out_specs=(
            P("row", "col"),
            P("row", "col"),
            P("col", "row", None, None),
            P("row", "col", None, None),
        ),
        check_vma=False,
    )
```

```python
import functools

import jax
import jax.numpy as jnp
from jax import lax
from jax.experimental import pallas as pl
from jax.experimental.pallas import tpu as pltpu
from jax.sharding import PartitionSpec as P

gelu_scale = 0.7978845608028654
gelu_cubic = 0.044715

CHUNKS = 3
PARTS = 2
DELAY = 2
PIECES = 4
VMEM_BYTES = 64 * 2**20 - 600 * 2**10


def gelu_pair(pre_act):
    inner_arg = gelu_scale * (pre_act + gelu_cubic * pre_act * pre_act * pre_act)
    tanh_value = jnp.tanh(inner_arg)
    activated = 0.5 * pre_act * (1.0 + tanh_value)
    derivative = 0.5 * (1.0 + tanh_value) + 0.5 * pre_act * (
        1.0 - tanh_value * tanh_value
    ) * gelu_scale * (1.0 + 3.0 * gelu_cubic * pre_act * pre_act)
    return (activated, derivative)


def divisor(total, most):
    return max(size for size in range(1, most + 1) if total % size == 0)


def params():
    return pltpu.CompilerParams(
        vmem_limit_bytes=VMEM_BYTES, dimension_semantics=("arbitrary",)
    )


def groups_of(count, width):
    return [list(range(at, min(at + width, count))) for at in range(0, count, width)]


ANY = pl.BlockSpec(memory_space=pl.ANY)


def view_spec(view, blocks, index):
    array, offset, tokens = view
    assert offset % tokens == 0
    shape = (array.shape[0], blocks, tokens, array.shape[3])
    return pl.BlockSpec(shape, lambda i, *refs: (0, index(i), offset // tokens, 0))


def chosen_copies(choices, refs, target, sems):
    copies = []
    at = 0
    for half, lane in enumerate(choices):
        for part, arrays in enumerate(lane):
            blocks = arrays[0].shape[0]
            for place in range(len(arrays)):
                copies.append(
                    (
                        half,
                        place,
                        pltpu.make_async_copy(
                            refs[at],
                            target.at[half, pl.ds(part * blocks, blocks)],
                            sems.at[half, part],
                        ),
                    )
                )
                at += 1
    return copies


def fetch(copies, position_ref):
    for act in ("start", "wait"):
        for half, place, copy in copies:

            @pl.when(position_ref[half] == place)
            def _(copy=copy, act=act):
                getattr(copy, act)()


def product_kernel(
    name, panel, values, index, position, out_shape, out_spec, work, after, resident, sums=None
):
    flops = 2**35 if isinstance(panel, list) else 2**20
    rows, slots, side = values.shape[:3]
    per = divisor(rows, max(1, 48 // slots))
    chosen = isinstance(panel, list)
    flat = [array for lane in panel for arrays in lane for array in arrays] if chosen else []
    if chosen:
        half_tokens = flat[0].shape[1]
        all_blocks = sum(arrays[0].shape[0] for arrays in panel[0])
        panel_shape = (len(panel), all_blocks, half_tokens, side)
        panel_specs, panel_operands = [ANY] * len(flat), flat
        out_specs = [out_spec(per), ANY]
        out_shapes = [out_shape, jax.ShapeDtypeStruct(panel_shape, jnp.bfloat16)]
        scratch = [
            pltpu.VMEM(panel_shape, jnp.bfloat16),
            pltpu.SemaphoreType.DMA((len(panel), len(panel[0]))),
            pltpu.SemaphoreType.DMA(()),
        ]
    else:
        blocks = panel[0].shape[1]
        spec = view_spec(panel, blocks, lambda i: 0) if resident else view_spec(panel, per, lambda i: i)
        panel_specs, panel_operands = [spec], [panel[0]]
        out_specs, out_shapes, scratch = [out_spec(per)], [out_shape], []
    if sums is not None:
        scratch.append(pltpu.VMEM(sums, jnp.float32))
    total = 2 * flat[0].shape[1] if chosen else panel[0].shape[0] * panel[2]
    last_step = rows // per - 1

    def body(index_ref, position_ref, value_ref, *refs):
        step = pl.program_id(0)
        total_ref = None
        if sums is not None:
            refs, total_ref = refs[:-1], refs[-1]
        if chosen:
            panel_refs = refs[: len(flat)]
            out_ref, kept_ref, held, sems, kept_sem = refs[len(flat) + len(after) :]
            keep = pltpu.make_async_copy(held, kept_ref, kept_sem)

            @pl.when(step == 0)
            def _():
                fetch(chosen_copies(panel, panel_refs, held, sems), position_ref)
                keep.start()

            def read(block, local):
                at = step * per + local if block is None else block
                return held[:, at].reshape(total, side)

        else:
            panel_ref, out_ref = refs[0], refs[1 + len(after)]

            def read(block, local):
                at = local if block is None else block
                return panel_ref[:, at].reshape(total, side)

        work(step, per, read, value_ref, index_ref, out_ref, total_ref)
        if chosen:

            @pl.when(step == last_step)
            def _():
                keep.wait()

    made = pl.pallas_call(
        body,
        grid_spec=pltpu.PrefetchScalarGridSpec(
            num_scalar_prefetch=2,
            grid=(rows // per,),
            in_specs=[pl.BlockSpec((per, slots, side, side), lambda i, *refs: (i, 0, 0, 0))]
            + panel_specs
            + [ANY] * len(after),
            out_specs=out_specs,
            scratch_shapes=scratch,
        ),
        out_shape=out_shapes,
        compiler_params=params(),
        cost_estimate=pl.CostEstimate(flops=flops, bytes_accessed=2**20, transcendentals=0),
        name=name,
    )(index, position, values, *panel_operands, *after)
    return made if chosen else made[0]


def spread(panel, values, index, position, out_blocks, out_groups, total, dtype, after=()):
    rows, slots, side = values.shape[:3]
    narrow = dtype != jnp.float32
    shape = (out_groups, out_blocks, total // out_groups, side)

    def work(step, per, read, value_ref, index_ref, out_ref, total_ref):
        total_ref = total_ref if narrow else out_ref

        @pl.when(step == 0)
        def _():
            total_ref[...] = jnp.zeros_like(total_ref)

        for local in range(per):
            source = read(None, local)
            for group in groups_of(slots, 2):
                weights = jnp.concatenate([value_ref[local, s] for s in group], axis=1)
                product = jnp.dot(source, weights, preferred_element_type=jnp.float32)
                for at, s in enumerate(group):
                    block = index_ref[(step * per + local) * slots + s]
                    piece = product[:, at * side : (at + 1) * side]
                    total_ref[:, block] += piece.reshape(out_groups, total // out_groups, side)

        if narrow:

            @pl.when(step == rows // per - 1)
            def _():
                for block in range(out_blocks):
                    out_ref[:, block] = total_ref[:, block].astype(dtype)

    return product_kernel(
        "spread",
        panel,
        values,
        index,
        position,
        jax.ShapeDtypeStruct(shape, dtype),
        lambda per: pl.BlockSpec(shape, lambda i, *refs: (0, 0, 0, 0)),
        work,
        list(after),
        False,
        shape if narrow else None,
    )


def collect(panel, values, index, position, out_groups, total, dtype, after=()):
    rows, slots, side = values.shape[:3]
    tokens = total // out_groups

    def work(step, per, read, value_ref, index_ref, out_ref, total_ref):
        for local in range(per):
            picked = [
                read(index_ref[(step * per + local) * slots + s], local) for s in range(slots)
            ]
            weights = jnp.concatenate([value_ref[local, s] for s in range(slots)], axis=1)
            summed = lax.dot_general(
                jnp.concatenate(picked, axis=1),
                weights,
                (((1,), (1,)), ((), ())),
                preferred_element_type=jnp.float32,
            )
            out_ref[:, local] = summed.reshape(out_groups, tokens, side).astype(dtype)

    return product_kernel(
        "collect",
        panel,
        values,
        index,
        position,
        jax.ShapeDtypeStruct((out_groups, rows, tokens, side), dtype),
        lambda per: pl.BlockSpec((out_groups, per, tokens, side), lambda i, *refs: (0, i, 0, 0)),
        work,
        list(after),
        True,
    )


def block_grads(lefts, rights, index, slots, after=(), flops=2**20):
    side = lefts[0][0].shape[3]
    rows = lefts[0][0].shape[1]
    per = divisor(rows, max(1, 24 // slots))
    count = len(lefts)

    def flat(piece):
        return piece.reshape(piece.shape[0] * piece.shape[1], side)

    def body(index_ref, *refs):
        left_refs, right_refs, out_ref = refs[:count], refs[count : 2 * count], refs[-1]
        step = pl.program_id(0)
        for local in range(per):
            left = jnp.concatenate([flat(ref[:, local]) for ref in left_refs], axis=0)
            turned = left.T
            for group in groups_of(slots, 2):
                columns = []
                for s in group:
                    block = index_ref[(step * per + local) * slots + s]
                    columns.append(
                        jnp.concatenate([flat(ref[:, block]) for ref in right_refs], axis=0)
                    )
                product = jnp.dot(
                    turned,
                    jnp.concatenate(columns, axis=1),
                    preferred_element_type=jnp.float32,
                )
                for at, s in enumerate(group):
                    out_ref[local, s] = product[:, at * side : (at + 1) * side].astype(
                        out_ref.dtype
                    )

    left_specs = [view_spec(view, per, lambda i: i) for view in lefts]
    right_specs = [view_spec(view, view[0].shape[1], lambda i: 0) for view in rights]
    return pl.pallas_call(
        body,
        grid_spec=pltpu.PrefetchScalarGridSpec(
            num_scalar_prefetch=1,
            grid=(rows // per,),
            in_specs=left_specs + right_specs + [ANY] * len(after),
            out_specs=pl.BlockSpec((per, slots, side, side), lambda i, *refs: (i, 0, 0, 0)),
        ),
        out_shape=jax.ShapeDtypeStruct((rows, slots, side, side), jnp.bfloat16),
        compiler_params=params(),
        cost_estimate=pl.CostEstimate(flops=flops, bytes_accessed=2**20, transcendentals=0),
        name="block_grads",
    )(index, *[v[0] for v in lefts], *[v[0] for v in rights], *after)


def add_shares(shares, after):
    devices, blocks, _, side = shares[0].shape
    per = divisor(blocks, 4)
    own = sum(array.shape[2] for array in shares)

    def body(*refs):
        out_ref = refs[-1]
        at = 0
        for ref in refs[: len(shares)]:
            tokens = ref.shape[2]
            for block in range(per):
                total = ref[0, block].astype(jnp.float32)
                for device in range(1, devices):
                    total = total + ref[device, block].astype(jnp.float32)
                out_ref[at : at + tokens, block * side : (block + 1) * side] = total.astype(
                    out_ref.dtype
                )
            at += tokens

    return pl.pallas_call(
        body,
        grid=(blocks // per,),
        in_specs=[
            pl.BlockSpec((devices, per, a.shape[2], side), lambda i: (0, i, 0, 0)) for a in shares
        ]
        + [ANY] * len(after),
        out_specs=pl.BlockSpec((own, per * side), lambda i: (0, i)),
        out_shape=jax.ShapeDtypeStruct((own, blocks * side), jnp.bfloat16),
        compiler_params=params(),
        cost_estimate=pl.CostEstimate(flops=2**20, bytes_accessed=2**20, transcendentals=0),
        name="add_shares",
    )(*shares, *after)


def col_step(position, lanes, last, rows, after):
    side = 128
    size = rows // PIECES
    operands, out_shapes, plan = [], [], []

    def operand(array):
        if array is None:
            return None
        operands.append(array)
        return len(operands) - 1

    def result(dtype):
        out_shapes.append(jax.ShapeDtypeStruct((rows, side), dtype))
        return len(out_shapes) - 1

    for lane in lanes:
        jobs = {}
        for place, job in lane["jobs"].items():
            jobs[place] = (job[0],) if len(job) == 1 else (job[0], operand(job[1])) + job[2:]
        plan.append(
            {
                "jobs": jobs,
                "kind": lane["kind"],
                "arrived": operand(lane["arrived"]),
                "saved": operand(lane["saved"]) if lane["kind"] == "grad" else None,
                "out": result(jnp.bfloat16),
                "kept": result(jnp.float32) if lane["kind"] == "pre" else None,
            }
        )
    n_in = len(operands)
    n_out = len(out_shapes)

    def body(position_ref, *refs):
        ins, outs = refs[:n_in], refs[n_in + len(after) : n_in + len(after) + n_out]
        arrived, terms, third, ready, load_sem, store_sem = refs[n_in + len(after) + n_out :]

        def loads(which, lane, place, piece):
            span = pl.ds(piece * size, size)
            job = lane["jobs"][place]

            def load(source, target, kind):
                return pltpu.make_async_copy(
                    source, target.at[which, span], load_sem.at[which, kind, piece]
                )

            if job[0] == "fresh":
                return [load(ins[job[1]].at[span], ready, 0)]
            if job[0] == "on":
                return [load(ins[lane["arrived"]].at[span], ready, 0)]
            array, half, part = job[1:]
            own = pl.ds(part * rows + piece * size, size)
            copies = [load(ins[array].at[half, own], terms, 0)]
            if place > 0:
                copies.append(load(ins[lane["arrived"]].at[span], arrived, 1))
            if place == last and lane["kind"] == "grad":
                copies.append(load(ins[lane["saved"]].at[span], third, 2))
            return copies

        def stores(which, lane, place, piece):
            span = pl.ds(piece * size, size)
            copies = [
                pltpu.make_async_copy(
                    ready.at[which, span], outs[lane["out"]].at[span], store_sem.at[which, 0, piece]
                )
            ]
            if place == last and lane["kind"] == "pre":
                copies.append(
                    pltpu.make_async_copy(
                        third.at[which, span],
                        outs[lane["kept"]].at[span],
                        store_sem.at[which, 1, piece],
                    )
                )
            return copies

        def each(act):
            for which, lane in enumerate(plan):
                for place in lane["jobs"]:

                    @pl.when(position_ref[which] == place)
                    def _(which=which, lane=lane, place=place):
                        act(which, lane, place)

        def start_all(which, lane, place):
            for piece in range(PIECES):
                for copy in loads(which, lane, place, piece):
                    copy.start()

        def work_all(which, lane, place):
            for piece in range(PIECES):
                for copy in loads(which, lane, place, piece):
                    copy.wait()
                span = pl.ds(piece * size, size)
                if lane["jobs"][place][0] == "sum":
                    total = terms[which, span]
                    if place > 0:
                        total = total + arrived[which, span].astype(jnp.float32)
                    if place == last and lane["kind"] == "pre":
                        third[which, span] = total
                        total = gelu_pair(total)[0]
                    elif place == last:
                        total = total * gelu_pair(third[which, span])[1]
                    ready[which, span] = total.astype(jnp.bfloat16)
                for copy in stores(which, lane, place, piece):
                    copy.start()

        def wait_all(which, lane, place):
            for piece in range(PIECES):
                for copy in stores(which, lane, place, piece):
                    copy.wait()

        each(start_all)
        each(work_all)
        each(wait_all)

    made = pl.pallas_call(
        body,
        grid_spec=pltpu.PrefetchScalarGridSpec(
            num_scalar_prefetch=1,
            grid=(1,),
            in_specs=[ANY] * (n_in + len(after)),
            out_specs=[ANY] * n_out,
            scratch_shapes=[
                pltpu.VMEM((2, rows, side), jnp.bfloat16),
                pltpu.VMEM((2, rows, side), jnp.float32),
                pltpu.VMEM((2, rows, side), jnp.float32),
                pltpu.VMEM((2, rows, side), jnp.bfloat16),
                pltpu.SemaphoreType.DMA((2, 3, PIECES)),
                pltpu.SemaphoreType.DMA((2, 2, PIECES)),
            ],
        ),
        out_shape=out_shapes,
        compiler_params=params(),
        cost_estimate=pl.CostEstimate(flops=2**20, bytes_accessed=2**20, transcendentals=0),
        name="col_step",
    )(position, *operands, *after)
    return [
        (made[lane["out"]], None if lane["kept"] is None else made[lane["kept"]]) for lane in plan
    ]


def in_order(arrays, after):
    def body(*refs):
        pass

    return pl.pallas_call(
        body,
        in_specs=[ANY] * (len(arrays) + len(after)),
        out_specs=[ANY] * len(arrays),
        out_shape=[jax.ShapeDtypeStruct(a.shape, a.dtype) for a in arrays],
        input_output_aliases={k: k for k in range(len(arrays))},
        cost_estimate=pl.CostEstimate(flops=1024, bytes_accessed=1024, transcendentals=0),
        compiler_params=pltpu.CompilerParams(vmem_limit_bytes=VMEM_BYTES),
        name="in_order",
    )(*arrays, *after)


def link_order(items, last):
    sums, results, slot, sum_turn = [], [], 0, True
    while len(results) < items:
        more_sums = len(sums) < items
        can_pass = len(results) < len(sums) and slot > sums[len(results)] + DELAY * last
        if more_sums and (len(sums) < items // 2 or sum_turn or not can_pass):
            sums.append(slot)
            sum_turn = False
        elif can_pass:
            results.append(slot)
            sum_turn = True
        slot += 1
    return sums, results


def shards(inputs, first_values, first_blocks, second_values, second_blocks, cotangent):
    n_row, n_col = lax.axis_size("row"), lax.axis_size("col")
    last = n_col - 1
    tiles, first_slots, side = first_values.shape[:3]
    hidden, second_slots = second_values.shape[:2]
    own = inputs.shape[0]
    chunks = divisor(own // 16, CHUNKS)
    parts = divisor(hidden, PARTS)
    part_blocks = hidden // parts
    rows = own // chunks
    total = rows * n_row
    item_rows = part_blocks * total // 2

    first_index = (first_blocks - lax.axis_index("row") * hidden).reshape(-1)
    second_index = (second_blocks - lax.axis_index("col") * tiles).reshape(-1)
    place = lax.axis_index("col").astype(jnp.int32)
    position = jnp.stack([place, last - place])
    result_place = jnp.stack([place, place])

    def by_block(array):
        return array.reshape(own, tiles, side).transpose(1, 0, 2)

    first = by_block(inputs)
    opening = lax.all_gather(first[:, :rows], "row")
    input_views = [(opening, 0, rows)]
    if chunks > 1:
        others = lax.all_gather(first[:, rows:], "row")
        input_views += [(others, at * rows, rows) for at in range(chunks - 1)]
    gathered = lax.all_gather(by_block(cotangent), "row")
    grad_views = [(gathered, at * rows, rows) for at in range(chunks)]

    items = 2 * chunks * parts
    sum_slots, result_slots = link_order(items, last)
    steps = result_slots[-1] + DELAY * (last - 1) + 1

    terms = {}
    panels = {}
    products = {}
    made = [{}, {}]
    kept = [{}, {}]
    arrived = [{}, {}]
    halves = (1, 0)
    up = [(k, k + 1) for k in range(last)]
    down = [(last - k, last - k - 1) for k in range(last)]

    def job(direction, step, k):
        slot = step - DELAY * k
        if slot in sum_slots:
            item = sum_slots.index(slot)
            return ("sum", terms[item // parts], halves[direction], item % parts)
        if slot in result_slots and k < last:
            item = result_slots.index(slot)
            if k > 0:
                return ("on",)
            return ("fresh", made[1 - direction][sum_slots[item] + DELAY * last])
        return None

    def make_terms(chunk, after):
        if chunk < chunks:
            result = spread(
                input_views[chunk], first_values, first_index, position, hidden, 2, total,
                jnp.float32, after,
            )
        else:
            result = collect(
                grad_views[chunk - chunks], second_values, second_index, position, 2, total,
                jnp.float32, after,
            )
        terms[chunk] = result.reshape(2, hidden * total // 2, side)
        return result

    def make_product(chunk, after):
        choices = []
        for half in range(2):
            lane = halves.index(half)
            pieces = []
            for part in range(parts):
                item = chunk * parts + part
                arrays = [made[lane][sum_slots[item] + DELAY * last]] + [
                    arrived[1 - lane][result_slots[item] + DELAY * (hop - 1)]
                    for hop in range(1, n_col)
                ]
                by_place = arrays if lane == 1 else arrays[::-1]
                pieces.append([a.reshape(part_blocks, total // 2, side) for a in by_place])
            choices.append(pieces)
        if chunk < chunks:
            result = spread(
                choices, second_values, second_index, result_place, tiles, n_row, total,
                jnp.bfloat16, after,
            )
        else:
            result = collect(
                choices, first_values, first_index, result_place, n_row, total, jnp.bfloat16, after
            )
        panels[chunk] = (result[1], 0, total // 2)
        products[chunk] = result[0]
        return result[0]

    def make_second_grad(after):
        products["second"] = block_grads(
            [panels[c] for c in range(chunks)], grad_views, second_index, second_slots, after
        )
        return products["second"]

    queue = {}
    for chunk in range(1, 2 * chunks):
        queue.setdefault(sum_slots[chunk * parts] - 1, []).append(
            functools.partial(make_terms, chunk)
        )
    for chunk in range(2 * chunks):
        ready = result_slots[(chunk + 1) * parts - 1] + DELAY * last
        ready += ready >= result_slots[-1]
        ready = min(ready, steps + DELAY - 1)
        queue.setdefault(ready, []).append(functools.partial(make_product, chunk))
        if chunk == chunks - 1:
            queue.setdefault(steps + DELAY - 1, []).append(make_second_grad)

    before = [make_terms(0, ())]
    mark = []
    for step in range(steps):
        lanes = []
        for direction in range(2):
            jobs = {k: job(direction, step, k) for k in range(n_col)}
            jobs = {k: found for k, found in jobs.items() if found is not None}
            kind, saved, last_item = None, None, None
            if last in jobs:
                last_item = sum_slots.index(step - DELAY * last)
                kind = "pre" if last_item < items // 2 else "grad"
                saved = kept[direction].get(last_item - items // 2)
            lanes.append(
                {
                    "jobs": jobs,
                    "kind": kind,
                    "saved": saved,
                    "arrived": arrived[direction].get(step - DELAY),
                }
            )
        if any(found != ("on",) for lane in lanes for found in lane["jobs"].values()):
            for direction, (out, pre) in enumerate(
                col_step(position, lanes, last, item_rows, before + mark)
            ):
                made[direction][step] = out
                if pre is not None:
                    kept[direction][last_item] = pre
        else:
            held = in_order([lane["arrived"] for lane in lanes], before + mark)
            for direction in range(2):
                arrived[direction][step - DELAY] = made[direction][step] = held[direction]
        before = []
        mark = [made[0][step]]
        for direction, pairs in enumerate((up, down)):
            pairs = [pairs[k] for k in lanes[direction]["jobs"] if k < last]
            if pairs:
                arrived[direction][step] = lax.ppermute(made[direction][step], "col", pairs)
        for make in queue.get(step, []):
            before.append(make(mark))
    for step in range(steps, steps + DELAY):
        held = in_order([arrived[direction][step - DELAY] for direction in range(2)], before + mark)
        for direction in range(2):
            arrived[direction][step - DELAY] = held[direction]
        before, mark = [], [held[0]]
        for make in queue.get(step, []):
            before.append(make(mark + before[-1:]))

    shares = []
    for chunk in range(2 * chunks):
        product = products[chunk]
        if shares:
            (product,) = in_order([product], shares[-1:])
        shares.append(lax.all_to_all(product, "row", 0, 0))
    first_grad = block_grads(
        input_views,
        [panels[chunks + c] for c in range(chunks)],
        first_index,
        first_slots,
        [product],
        2**38,
    )
    outputs = add_shares(shares[:chunks], [first_grad])
    input_grad = add_shares(shares[chunks:], [first_grad])
    return (outputs, input_grad, first_grad, products["second"])


def solution(mesh):
    placed = (
        P("row", "col"),
        P("col", "row", None, None),
        P("col", "row"),
        P("row", "col", None, None),
        P("row", "col"),
        P("row", "col"),
    )
    return jax.shard_map(
        shards,
        mesh=mesh,
        in_specs=placed,
        out_specs=(
            P("row", "col"),
            P("row", "col"),
            P("col", "row", None, None),
            P("row", "col", None, None),
        ),
        check_vma=False,
    )
```
